128 devices in a mesh: grp: 8 (over y, core), sub: 16 (over x, z).
Axes of the slice: x: 4, y: 4, z: 4, core: 2. Of those that a mesh axis runs over, the one named last changes fastest.
Arguments:
- points: bfloat16 [8192, 1024], P(('grp', 'sub')), may hold values from -6 to 6
- point_cluster: int32 [8192], P(('grp', 'sub')), may hold values from 0 to 262143, as said below
- candidates: int32 [8192, 128], P(('grp', 'sub')), may hold values from 0 to 262143, as said below
- old_fine: bfloat16 [262144, 1024], P(('grp', 'sub')), may hold values from -6 to 6
- fine_parent: int32 [262144], P(('grp', 'sub')), may hold values from 0 to 16383, as said below
- old_middle: bfloat16 [16384, 1024], P('grp'), may hold values from -6 to 6
- middle_parent: int32 [16384], P('grp'), may hold values from 0 to 1023
- old_top: bfloat16 [1024, 1024], replicated, may hold values from -6 to 6
Outputs:
- new_fine: bfloat16 [262144, 1024], P(('grp', 'sub'))
- new_middle: bfloat16 [16384, 1024], P('grp')
- new_top: bfloat16 [1024, 1024], replicated
- candidate_sq_distance: float32 [8192, 128], P(('grp', 'sub'))
The draws below stay inside these ranges and needn't reach their ends.
Inputs may be any that keep to these rules, and one draw needn't show every extreme that they name: `point_cluster`: Level-1 centroids are held in slices of 2048 rows, slice f on the device of flat index f over grp then sub. Among the 64 points of one device, at most 3 belong to the centroids of any one slice; in every draw some slice receives exactly 3 from every device. `candidates`: candidate j of a point held by a device in group g of grp lies in the slice of the device (g, j mod 16). `fine_parent`: A level-1 centroid held in group g of grp has its parent among the level-2 centroids g * 16384 / 8 to (g + 1) * 16384 / 8 - 1. Split these into 16 equal consecutive shares: of the 2048 level-1 centroids of one slice, exactly 2048 / 16 have their parent in each share.
All inputs are finite; a program needn't handle non-finite values.
Results may differ from the reference program's by a relative error of at most 0.018.
Values may be sent and summed in bfloat16 or wider, within the bound.
No kernel may reach another device: no remote copies, remote signals or barrier semaphores. Data moves between devices by JAX's collectives and lax.ppermute only.
A program may use at most 192 MiB of HBM per device.

```python
from functools import partial
import jax
import jax.numpy as jnp
from jax import lax

D = 1024
K1_DEV = 2048
K2 = 16384
K3 = 1024
CANDS = 128
CAP = 3
ROWS = 64
K1 = 262144
NPTS = 8192
N_GRP = 8
N_SUB = 16


def draw_point_cluster(key, part):
    key = jax.random.fold_in(key, 101)
    blocks = N_GRP * N_SUB
    slots = blocks * CAP
    keys = jax.random.split(key, 6)
    baseline_score = jax.random.randint(keys[0], (blocks, slots), 0, 1024)
    frequent_centroid = jax.random.randint(keys[1], (blocks,), 0, 4)
    slot_holder_ids = jnp.arange(slots, dtype=jnp.int32) // CAP
    extra_reward = frequent_centroid[slot_holder_ids] * 1024
    hot_all = jax.random.randint(keys[2], (), 0, blocks)
    hot_block = jax.random.randint(keys[3], (blocks,), 0, blocks)
    ranking_score = baseline_score + extra_reward[None, :]
    ranking_score = ranking_score + jnp.where(slot_holder_ids[None, :] == hot_all, 16384, 0)
    ranking_score = ranking_score + jnp.where(slot_holder_ids[None, :] == hot_block[:, None], 8192, 0)
    ranking_score = ranking_score * slots + jnp.arange(slots, dtype=jnp.int32)[None, :]
    chosen = lax.top_k(ranking_score, ROWS)[1]
    shuffle = jax.random.randint(keys[4], (blocks, ROWS), 0, 65536) * ROWS + jnp.arange(ROWS, dtype=jnp.int32)[None, :]
    order = jnp.argsort(shuffle, axis=1, stable=True)
    chosen = jnp.take_along_axis(chosen, order, axis=1)
    owners = chosen // CAP
    local_ids = jax.random.randint(keys[5], (blocks, ROWS), 0, K1_DEV)
    return (owners * K1_DEV + local_ids).reshape(-1).astype(jnp.int32)


def draw_candidates(key, part):
    key = jax.random.fold_in(key, 202)
    total = ROWS * N_GRP * N_SUB
    row_index = jnp.arange(total, dtype=jnp.int32)
    group = row_index // ROWS // N_SUB
    column = jnp.arange(CANDS, dtype=jnp.int32)
    owners = group[:, None] * N_SUB + column[None, :] % N_SUB
    local_ids = jax.random.randint(key, (total, CANDS), 0, K1_DEV)
    return (owners * K1_DEV + local_ids).astype(jnp.int32)


def draw_fine_parent(key, part):
    key = jax.random.fold_in(key, 303)
    blocks = N_GRP * N_SUB
    keys = jax.random.split(key, 2)
    per_group = K2 // N_GRP
    share_size = per_group // N_SUB
    per_share = K1_DEV // N_SUB
    base_share = jnp.arange(K1_DEV, dtype=jnp.int32) // per_share
    shuffle = jax.random.randint(keys[0], (blocks, K1_DEV), 0, 65536) * K1_DEV + jnp.arange(K1_DEV, dtype=jnp.int32)[None, :]
    order = jnp.argsort(shuffle, axis=1, stable=True)
    shares = base_share[order]
    within = jax.random.randint(keys[1], (blocks, K1_DEV), 0, share_size)
    group = jnp.arange(blocks, dtype=jnp.int32)[:, None] // N_SUB
    return (group * per_group + shares * share_size + within).reshape(-1).astype(jnp.int32)


def touch_ends(array, own_key, smallest, high):
    dims = array.shape
    place = [jax.random.randint(jax.random.fold_in(own_key, axis), (), 0, dims[axis]) for axis in range(len(dims))]
    array = array.at[tuple(place)].set(smallest)
    longest = dims.index(max(dims))
    place[longest] = (place[longest] + 1) % dims[longest]
    return array.at[tuple(place)].set(high)


def steps_of(rng, dims, cuts, low, high):
    loudness = 1.0
    for dim, blocks in cuts:
        draws = jax.random.uniform(jax.random.fold_in(jax.random.fold_in(rng, 6), dim), (blocks,), jnp.float32, low / len(cuts), high / len(cuts))
        loudness = loudness * jnp.repeat(jnp.exp(draws), dims[dim] // blocks).reshape((-1,) + (1,) * (len(dims) - 1 - dim))
    return loudness


def bell_draw(key, shape, spread, bound, shards=(), held_as=jnp.bfloat16):
    level = steps_of(key, shape, shards, -0.22, 0.18) if shards else 1.0
    drawn = jax.random.normal(key, shape, jnp.float32) * spread * level
    return jnp.minimum(jnp.maximum(drawn, -bound), bound).astype(held_as)


def setup_inputs(seed: int = 0) -> dict:
    seeds = jax.random.split(jax.random.key(seed), 9)
    return {
        "points": bell_draw(seeds[0], (NPTS, D), 1.0, 6.0, ((0, 128),)),
        "point_cluster": draw_point_cluster(jax.random.fold_in(seeds[8], 71), 0),
        "candidates": draw_candidates(jax.random.fold_in(seeds[8], 71), 0),
        "old_fine": bell_draw(seeds[3], (K1, D), 1.0, 6.0, ((0, 128),)),
        "fine_parent": draw_fine_parent(jax.random.fold_in(seeds[8], 71), 0),
        "old_middle": bell_draw(seeds[5], (K2, D), 1.0, 6.0, ((0, 8),)),
        "middle_parent": touch_ends(jax.random.randint(seeds[6], (K2,), 0, K3), jax.random.fold_in(seeds[6], 1), 0, K3 - 1).astype(jnp.int32),
        "old_top": bell_draw(seeds[7], (K3, D), 1.0, 6.0),
    }


def block_dist(centroids, pair):
    block_points, block_ids = pair
    picked = centroids[block_ids].astype(jnp.float32)
    gap = block_points.astype(jnp.float32)[:, None, :] - picked
    return jnp.mean(gap * gap, axis=-1)


def update_level(values, parents, olds, count):
    totals = jnp.zeros((count, values.shape[1]), jnp.float32).at[parents].add(values.astype(jnp.float32))
    members = jnp.zeros((count,), jnp.float32).at[parents].add(jnp.ones(parents.shape, jnp.float32))
    return ((totals + olds.astype(jnp.float32)) / (members + 1.0)[:, None]).astype(jnp.bfloat16)


def reference(points, point_cluster, candidates, old_fine, fine_parent, old_middle, middle_parent, old_top):
    new_fine = update_level(points, point_cluster, old_fine, K1)
    new_middle = update_level(new_fine, fine_parent, old_middle, K2)
    new_top = update_level(new_middle, middle_parent, old_top, K3)
    blocks = NPTS // ROWS
    dist_blocks = lax.map(partial(block_dist, old_fine), (points.reshape(blocks, ROWS, D), candidates.reshape(blocks, ROWS, CANDS)))
    return new_fine, new_middle, new_top, dist_blocks.reshape(NPTS, CANDS)
```

```python
import jax
import jax.numpy as jnp
from jax import lax
from jax.experimental import pallas as pl
from jax.experimental.pallas import tpu as pltpu
from jax.sharding import PartitionSpec as P

CAP = 3
LANES = 128
LANE_BITS = 7
ID_BASE = 64
LOW_LANE = 8
COUNT_LANE = 16
BOTH = ("grp", "sub")


def level_update(totals, members, olds):
    return ((totals + olds.astype(jnp.float32)) / (members + 1.0)[:, None]).astype(jnp.bfloat16)


def member_table(count, parents):
    return (jnp.arange(count, dtype=jnp.int32)[:, None] == parents[None, :]).astype(jnp.bfloat16)


def swap(blocks, axes):
    return lax.all_to_all(blocks, axes, split_axis=0, concat_axis=0, tiled=True)


def spread(block, axes):
    copies = lax.axis_size(axes)
    return swap(jnp.broadcast_to(block[None], (copies,) + block.shape), axes)


def distance_kernel(base_ref, points_ref, ids_ref, fine_ref, norms_ref, out_ref):
    rows, feat_dim = points_ref.shape
    fine_count = fine_ref.shape[0]
    block = points_ref[...]
    wide = block.astype(jnp.float32)
    point_norms = jnp.sum(wide * wide, axis=1, keepdims=True)
    cross = lax.dot_general(
        block, fine_ref[...], (((1,), (1,)), ((), ())), preferred_element_type=jnp.float32
    )
    local = ids_ref[...].reshape(rows, LANES) - base_ref[0]
    chunk = lax.shift_right_arithmetic(local, LANE_BITS)
    lane = jnp.bitwise_and(local, LANES - 1)
    picked = jnp.full((rows, LANES), 0.0, jnp.float32)
    for c in range(fine_count // LANES):
        here = slice(c * LANES, (c + 1) * LANES)
        scores = norms_ref[:, here] - 2.0 * cross[:, here]
        found = jnp.take_along_axis(scores, lane, axis=1)
        picked = jnp.where(chunk == c, found, picked)
    mine = jnp.logical_and(local >= 0, local < fine_count)
    total = jnp.maximum(picked + point_norms, 0.0) * (1.0 / feat_dim)
    out_ref[...] = jnp.where(mine, total, 0.0).reshape(out_ref.shape)


def candidate_parts(base, all_points, ids, old_fine, fine_norms):
    groups, row_count, cand_count = ids.shape
    fine_count, feat_dim = old_fine.shape
    per_step = 2
    return pl.pallas_call(
        distance_kernel,
        out_shape=jax.ShapeDtypeStruct((groups, row_count, cand_count), jnp.float32),
        grid_spec=pltpu.PrefetchScalarGridSpec(
            num_scalar_prefetch=1,
            grid=(groups // per_step,),
            in_specs=[
                pl.BlockSpec((per_step * row_count, feat_dim), lambda i, b: (i, 0)),
                pl.BlockSpec((per_step, row_count, cand_count), lambda i, b: (i, 0, 0)),
                pl.BlockSpec((fine_count, feat_dim), lambda i, b: (0, 0)),
                pl.BlockSpec((1, fine_count), lambda i, b: (0, 0)),
            ],
            out_specs=pl.BlockSpec((per_step, row_count, cand_count), lambda i, b: (i, 0, 0)),
        ),
        compiler_params=pltpu.CompilerParams(vmem_limit_bytes=40 * 1024 * 1024),
        cost_estimate=pl.CostEstimate(
            flops=2 * groups * row_count * fine_count * feat_dim,
            bytes_accessed=2 * (groups * row_count + fine_count) * feat_dim,
            transcendentals=0,
        ),
    )(base, all_points, ids, old_fine, fine_norms)


def per_device(
    points, point_cluster, candidates, old_fine, fine_parent, old_middle, middle_parent, old_top
):
    devices = lax.axis_size(BOTH)
    group_width = lax.axis_size("sub")
    share = lax.axis_index("sub")
    device = lax.axis_index(BOTH)
    row_count, feat_dim = points.shape
    fine_count = old_fine.shape[0]
    middle_count = old_middle.shape[0]
    top_count = old_top.shape[0]
    share_rows = middle_count // group_width
    top_rows = top_count // devices

    all_points = lax.all_gather(points, "sub", axis=0, tiled=True)

    middle_local = fine_parent - lax.axis_index("grp") * middle_count
    middle_table = member_table(middle_count, middle_local)
    middle_members = jnp.sum(middle_table, axis=1, dtype=jnp.float32).astype(jnp.int32)
    first = jnp.concatenate([candidates, middle_members.reshape(group_width, share_rows)], axis=0)
    firsts = spread(first, "sub")
    middle_totals = jnp.sum(firsts[:, row_count:, :], axis=0).astype(jnp.float32)

    owners = point_cluster // fine_count
    local_ids = point_cluster - owners * fine_count
    order = jnp.arange(row_count, dtype=jnp.int32)
    ahead = jnp.logical_and(owners[:, None] == owners[None, :], order[None, :] < order[:, None])
    ranks = jnp.sum(ahead.astype(jnp.int32), axis=1)
    lane = jnp.arange(feat_dim, dtype=jnp.int32)[None, :]
    id_rows = jnp.where(
        lane == ranks[:, None],
        (local_ids // ID_BASE + 1)[:, None],
        jnp.where(lane == LOW_LANE + ranks[:, None], (local_ids % ID_BASE)[:, None], 0),
    ).astype(jnp.bfloat16)
    share_parent = lax.dynamic_slice_in_dim(middle_parent, share * share_rows, share_rows)
    top_members = jnp.sum(member_table(top_count, share_parent), axis=1, dtype=jnp.float32)
    count_rows = jnp.pad(
        top_members.reshape(devices, top_rows).astype(jnp.bfloat16),
        ((0, 0), (COUNT_LANE, feat_dim - COUNT_LANE - top_rows)),
    )
    slot_count = CAP + 1
    every = jnp.arange(devices, dtype=jnp.int32)
    slots = jnp.concatenate(
        [owners * slot_count + ranks, owners * slot_count + CAP, every * slot_count + CAP]
    )
    payload = jnp.concatenate([points, id_rows, count_rows], axis=0)
    send_rows = jnp.dot(
        member_table(devices * slot_count, slots), payload, preferred_element_type=jnp.float32
    ).astype(jnp.bfloat16)
    got = swap(send_rows.reshape(devices, slot_count, feat_dim), BOTH)
    side = got[:, CAP, : COUNT_LANE + top_rows].astype(jnp.float32)
    got_high = side[:, :CAP].astype(jnp.int32)
    got_low = side[:, LOW_LANE : LOW_LANE + CAP].astype(jnp.int32)
    got_ids = jnp.where(got_high > 0, (got_high - 1) * ID_BASE + got_low, -1)
    got_ids = jnp.pad(got_ids, ((0, 0), (0, 1)), constant_values=-1).reshape(devices * slot_count)
    top_totals = jnp.sum(side[:, COUNT_LANE:], axis=0)

    fine_table = member_table(fine_count, got_ids)
    fine_sums = jnp.dot(
        fine_table, got.reshape(devices * slot_count, feat_dim), preferred_element_type=jnp.float32
    )
    fine_members = jnp.sum(fine_table, axis=1, dtype=jnp.float32)
    new_fine = level_update(fine_sums, fine_members, old_fine)

    middle_part = jnp.dot(middle_table, new_fine, preferred_element_type=jnp.float32).astype(
        jnp.bfloat16
    )
    parts = swap(middle_part.reshape(group_width, share_rows, feat_dim), "sub")
    share_totals = lax.dynamic_slice_in_dim(middle_totals, share, 1).reshape(share_rows)
    old_share = lax.dynamic_slice_in_dim(old_middle, share * share_rows, share_rows)
    new_share = level_update(
        jnp.sum(parts.astype(jnp.float32), axis=0), share_totals, old_share
    )
    new_middle = lax.all_gather(new_share, "sub", axis=0, tiled=True)

    middle_ids = jnp.arange(middle_count, dtype=jnp.int32)
    in_share = (middle_ids // share_rows == share)[:, None]
    scaled = middle_part.astype(jnp.float32) + jnp.where(
        in_share, old_middle.astype(jnp.float32), 0.0
    )
    scaled = scaled / (middle_totals.reshape(middle_count) + 1.0)[:, None]
    top_part = jnp.dot(
        member_table(top_count, middle_parent),
        scaled.astype(jnp.bfloat16),
        preferred_element_type=jnp.float32,
    )
    top_block = lax.psum_scatter(top_part, "grp", scatter_dimension=0, tiled=True)
    top_pieces = swap(top_block.reshape(group_width, top_rows, feat_dim), "sub")
    old_rows = lax.dynamic_slice_in_dim(old_top, device * top_rows, top_rows)
    new_rows = level_update(jnp.sum(top_pieces, axis=0), top_totals, old_rows)
    new_top = spread(new_rows, BOTH).reshape(top_count, feat_dim)

    wide_fine = old_fine.astype(jnp.float32)
    fine_norms = jnp.sum(wide_fine * wide_fine, axis=1)[None, :]
    base = (device * fine_count).reshape(1)
    found = candidate_parts(base, all_points, firsts[:, :row_count, :], old_fine, fine_norms)
    candidate_sq_distance = jnp.sum(swap(found, "sub"), axis=0)
    return (new_fine, new_middle, new_top, candidate_sq_distance)


def solution(mesh):
    placed = (
        P(BOTH, None),
        P(BOTH),
        P(BOTH, None),
        P(BOTH, None),
        P(BOTH),
        P("grp", None),
        P("grp"),
        P(),
    )
    return jax.shard_map(
        per_device,
        mesh=mesh,
        in_specs=placed,
        out_specs=(P(BOTH, None), P("grp", None), P(), P(BOTH, None)),
        check_vma=False,
    )
```

```python
import jax
import jax.numpy as jnp
from jax import lax
from jax.experimental import pallas as pl
from jax.experimental.pallas import tpu as pltpu
from jax.sharding import PartitionSpec as P

CAP = 3
LANES = 128
ID_BASE = 64
LOW_LANE = 8
COUNT_LANE = 16
FINE_STEP = 512
MIDDLE_STEP = 512
TOP_STEP = 512
EXACT = 256
BOTH = ("grp", "sub")


def level_update(totals, members, olds):
    return ((totals + olds.astype(jnp.float32)) / (members + 1.0)[:, None]).astype(jnp.bfloat16)


def member_table(count, parents):
    return (jnp.arange(count, dtype=jnp.int32)[:, None] == parents[None, :]).astype(jnp.bfloat16)


def swap(blocks, axes):
    return lax.all_to_all(blocks, axes, split_axis=0, concat_axis=0, tiled=True)


def spread(block, axes):
    copies = lax.axis_size(axes)
    return swap(jnp.broadcast_to(block[None], (copies,) + block.shape), axes)


def dot(left, right):
    return jnp.dot(left, right, preferred_element_type=jnp.float32)


def hits(count, first, parents):
    rows = lax.broadcasted_iota(jnp.int32, (count, parents.shape[1]), 0) + first
    return rows == parents


def quick_table(rows, first, parents):
    pieces = []
    for begin in range(0, rows, EXACT):
        near = parents - (first + begin)
        near = jnp.where(jnp.logical_and(near >= 0, near < EXACT), near, -1)
        near = near.astype(jnp.float32).astype(jnp.bfloat16)
        ids = lax.broadcasted_iota(jnp.int32, (EXACT, parents.shape[1]), 0)
        ids = ids.astype(jnp.float32).astype(jnp.bfloat16)
        pieces.append(jnp.where(ids == near, jnp.bfloat16(1), jnp.bfloat16(0)))
    return jnp.concatenate(pieces, axis=0)


def levels_kernel(
    got_ref,
    ids_ref,
    old_fine_ref,
    parent_ref,
    members_ref,
    old_share_ref,
    share_members_ref,
    share_parent_ref,
    top_parent_ref,
    fine_ref,
    middle_ref,
    top_ref,
    held,
    scaled,
    sent,
):
    step = pl.program_id(0)
    last = pl.num_programs(0) - 1
    fine_steps = held.shape[0] // FINE_STEP
    middle_steps = scaled.shape[0] // MIDDLE_STEP
    top_rows = top_ref.shape[0]
    store = pltpu.make_async_copy(held, fine_ref, sent)

    @pl.when(step < fine_steps)
    def _():
        first = pl.multiple_of(step * FINE_STEP, FINE_STEP)
        found = hits(FINE_STEP, first, ids_ref[...])
        members = jnp.sum(found.astype(jnp.float32), axis=1, keepdims=True)
        totals = dot(found.astype(jnp.bfloat16), got_ref[...])
        totals = totals + old_fine_ref[...].astype(jnp.float32)
        held[pl.ds(first, FINE_STEP), :] = (totals * (1.0 / (members + 1.0))).astype(jnp.bfloat16)

    @pl.when(step == fine_steps)
    def _():
        store.start()

    @pl.when(jnp.logical_and(step >= fine_steps, step < fine_steps + middle_steps))
    def _():
        first = pl.multiple_of((step - fine_steps) * MIDDLE_STEP, MIDDLE_STEP)
        part = dot(quick_table(MIDDLE_STEP, first, parent_ref[...]), held[...])
        middle_ref[...] = part.astype(jnp.bfloat16)
        weighted = part * (1.0 / (members_ref[...] + 1.0))
        scaled[pl.ds(first, MIDDLE_STEP), :] = weighted.astype(jnp.bfloat16)

    @pl.when(step >= fine_steps + middle_steps)
    def _():
        first = (step - fine_steps - middle_steps) * top_rows
        olds = old_share_ref[...].astype(jnp.float32)
        olds = (olds * (1.0 / (share_members_ref[...] + 1.0))).astype(jnp.bfloat16)
        own_table = quick_table(top_rows, first, share_parent_ref[...])
        table = quick_table(top_rows, first, top_parent_ref[...])
        top_ref[...] = dot(table, scaled[...]) + dot(own_table, olds)

    @pl.when(step == last)
    def _():
        store.wait()


def levels(got, ids, old_fine, parents, members, old_share, share_members, share_parent, top):
    fine_count, feat_dim = old_fine.shape
    middle_count = members.shape[0]
    top_parents, top_count = top
    share_rows = old_share.shape[0]
    slots = got.shape[0]
    fine_steps = fine_count // FINE_STEP
    middle_steps = middle_count // MIDDLE_STEP
    top_steps = top_count // TOP_STEP

    def fine_at(i):
        return (jnp.minimum(i, fine_steps - 1), 0)

    def middle_at(i):
        return (jnp.clip(i - fine_steps, 0, middle_steps - 1), 0)

    def top_at(i):
        return (jnp.maximum(i - fine_steps - middle_steps, 0), 0)

    def whole(i):
        return (0, 0)

    flops = 2 * feat_dim * (fine_count * slots + middle_count * (fine_count + top_count))
    return pl.pallas_call(
        levels_kernel,
        out_shape=(
            jax.ShapeDtypeStruct((fine_count, feat_dim), jnp.bfloat16),
            jax.ShapeDtypeStruct((middle_count, feat_dim), jnp.bfloat16),
            jax.ShapeDtypeStruct((top_count, feat_dim), jnp.float32),
        ),
        grid=(fine_steps + middle_steps + top_steps,),
        in_specs=[
            pl.BlockSpec((slots, feat_dim), whole),
            pl.BlockSpec((1, slots), whole),
            pl.BlockSpec((FINE_STEP, feat_dim), fine_at),
            pl.BlockSpec((1, fine_count), whole),
            pl.BlockSpec((MIDDLE_STEP, 1), middle_at),
            pl.BlockSpec((share_rows, feat_dim), whole),
            pl.BlockSpec((share_rows, 1), whole),
            pl.BlockSpec((1, share_rows), whole),
            pl.BlockSpec((1, middle_count), whole),
        ],
        out_specs=[
            pl.BlockSpec(memory_space=pl.ANY),
            pl.BlockSpec((MIDDLE_STEP, feat_dim), middle_at),
            pl.BlockSpec((TOP_STEP, feat_dim), top_at),
        ],
        scratch_shapes=[
            pltpu.VMEM((fine_count, feat_dim), jnp.bfloat16),
            pltpu.VMEM((middle_count, feat_dim), jnp.bfloat16),
            pltpu.SemaphoreType.DMA,
        ],
        compiler_params=pltpu.CompilerParams(vmem_limit_bytes=54 * 1024 * 1024),
        cost_estimate=pl.CostEstimate(
            flops=flops, bytes_accessed=18 * 1024 * 1024, transcendentals=0
        ),
    )(got, ids, old_fine, parents, members, old_share, share_members, share_parent, top_parents)


def distance_kernel(share_ref, rows_ref, fine_ref, norms_ref, out_ref):
    fine_count, feat_dim = fine_ref.shape
    rows = rows_ref.shape[0]
    block = rows_ref[:, :feat_dim]
    wide = block.astype(jnp.float32)
    point_norms = jnp.sum(wide * wide, axis=1, keepdims=True)
    cross = lax.dot_general(
        block, fine_ref[...], (((1,), (1,)), ((), ())), preferred_element_type=jnp.float32
    )
    places = rows_ref[:, feat_dim : feat_dim + 2 * LANES].astype(jnp.float32).astype(jnp.int32)
    chunk = places[:, :LANES]
    lane = places[:, LANES:]
    picked = jnp.zeros((rows, LANES), jnp.float32)
    for c in range(fine_count // LANES):
        here = slice(c * LANES, (c + 1) * LANES)
        scores = norms_ref[:, here] - 2.0 * cross[:, here]
        found = jnp.take_along_axis(scores, lane, axis=1)
        picked = jnp.where(chunk == c, found, picked)
    column = lax.broadcasted_iota(jnp.int32, (rows, LANES), 1)
    mine = jnp.bitwise_and(column, share_ref[1] - 1) == share_ref[0]
    total = jnp.maximum(picked + point_norms, 0.0) * (1.0 / feat_dim)
    out_ref[...] = jnp.where(mine, total, 0.0).reshape(out_ref.shape)


def candidate_parts(share, all_rows, old_fine, fine_norms, groups):
    row_count = all_rows.shape[0] // groups
    fine_count, feat_dim = old_fine.shape
    per_step = 2
    return pl.pallas_call(
        distance_kernel,
        out_shape=jax.ShapeDtypeStruct((groups, row_count, LANES), jnp.float32),
        grid_spec=pltpu.PrefetchScalarGridSpec(
            num_scalar_prefetch=1,
            grid=(groups // per_step,),
            in_specs=[
                pl.BlockSpec((per_step * row_count, all_rows.shape[1]), lambda i, s: (i, 0)),
                pl.BlockSpec((fine_count, feat_dim), lambda i, s: (0, 0)),
                pl.BlockSpec((1, fine_count), lambda i, s: (0, 0)),
            ],
            out_specs=pl.BlockSpec((per_step, row_count, LANES), lambda i, s: (i, 0, 0)),
        ),
        compiler_params=pltpu.CompilerParams(vmem_limit_bytes=40 * 1024 * 1024),
        cost_estimate=pl.CostEstimate(
            flops=2 * groups * row_count * fine_count * feat_dim,
            bytes_accessed=2 * (groups * row_count + fine_count) * feat_dim,
            transcendentals=0,
        ),
    )(share, all_rows, old_fine, fine_norms)


def per_device(
    points, point_cluster, candidates, old_fine, fine_parent, old_middle, middle_parent, old_top
):
    devices = lax.axis_size(BOTH)
    group_width = lax.axis_size("sub")
    share = lax.axis_index("sub")
    device = lax.axis_index(BOTH)
    row_count, feat_dim = points.shape
    fine_count = old_fine.shape[0]
    middle_count = old_middle.shape[0]
    top_count = old_top.shape[0]
    share_rows = middle_count // group_width
    top_rows = top_count // devices
    which = jnp.stack([share, jnp.int32(group_width)])

    owners = point_cluster // fine_count
    local_ids = point_cluster - owners * fine_count
    order = jnp.arange(row_count, dtype=jnp.int32)
    ahead = jnp.logical_and(owners[:, None] == owners[None, :], order[None, :] < order[:, None])
    ranks = jnp.sum(ahead.astype(jnp.int32), axis=1)
    lane = jnp.arange(feat_dim, dtype=jnp.int32)[None, :]
    id_rows = jnp.where(
        lane == ranks[:, None],
        (local_ids // ID_BASE + 1)[:, None],
        jnp.where(lane == LOW_LANE + ranks[:, None], (local_ids % ID_BASE)[:, None], 0),
    ).astype(jnp.bfloat16)
    share_parent = lax.dynamic_slice_in_dim(middle_parent, share * share_rows, share_rows)
    top_members = jnp.sum(member_table(top_count, share_parent), axis=1, dtype=jnp.float32)
    count_rows = jnp.pad(
        top_members.reshape(devices, top_rows).astype(jnp.bfloat16),
        ((0, 0), (COUNT_LANE, feat_dim - COUNT_LANE - top_rows)),
    )
    slot_count = CAP + 1
    every = jnp.arange(devices, dtype=jnp.int32)
    slots = jnp.concatenate(
        [owners * slot_count + ranks, owners * slot_count + CAP, every * slot_count + CAP]
    )
    payload = jnp.concatenate([points, id_rows, count_rows], axis=0)
    send_rows = dot(member_table(devices * slot_count, slots), payload).astype(jnp.bfloat16)
    got = swap(send_rows.reshape(devices, slot_count, feat_dim), BOTH)
    side = got[:, CAP, : COUNT_LANE + top_rows].astype(jnp.float32)
    got_high = side[:, :CAP].astype(jnp.int32)
    got_low = side[:, LOW_LANE : LOW_LANE + CAP].astype(jnp.int32)
    got_ids = jnp.where(got_high > 0, (got_high - 1) * ID_BASE + got_low, -1)
    got_ids = jnp.pad(got_ids, ((0, 0), (0, 1)), constant_values=-1)
    top_totals = jnp.sum(side[:, COUNT_LANE:], axis=0)

    place = candidates % fine_count
    wide_rows = jnp.concatenate(
        [points, (place // LANES).astype(jnp.bfloat16), (place % LANES).astype(jnp.bfloat16)],
        axis=1,
    )
    all_rows = lax.all_gather(wide_rows, "sub", axis=0, tiled=True)

    middle_local = fine_parent - lax.axis_index("grp") * middle_count
    middle_table = member_table(middle_count, middle_local)
    middle_members = jnp.sum(middle_table, axis=1, dtype=jnp.float32)
    middle_members = middle_members.reshape(group_width, share_rows)
    apart = 1
    while apart < group_width:
        partners = [(i, i ^ apart) for i in range(group_width)]
        middle_members = middle_members + lax.ppermute(middle_members, "sub", partners)
        apart *= 2

    old_share = lax.dynamic_slice_in_dim(old_middle, share * share_rows, share_rows)
    share_totals = lax.dynamic_slice_in_dim(middle_members, share, 1).reshape(share_rows)
    new_fine, middle_part, top_part = levels(
        got.reshape(devices * slot_count, feat_dim),
        got_ids.reshape(1, devices * slot_count),
        old_fine,
        middle_local[None, :],
        middle_members.reshape(middle_count, 1),
        old_share,
        share_totals[:, None],
        share_parent[None, :],
        (middle_parent[None, :], top_count),
    )

    parts = swap(middle_part.reshape(group_width, share_rows, feat_dim), "sub")
    wide_fine = old_fine.astype(jnp.float32)
    fine_norms = jnp.sum(wide_fine * wide_fine, axis=1)[None, :]
    found = candidate_parts(which, all_rows, old_fine, fine_norms, group_width)
    parts, found = lax.optimization_barrier((parts, found))
    new_share = level_update(jnp.sum(parts.astype(jnp.float32), axis=0), share_totals, old_share)
    new_middle = lax.all_gather(new_share, "sub", axis=0, tiled=True)

    top_block = lax.psum_scatter(top_part, "grp", scatter_dimension=0, tiled=True)
    piece_rows = top_rows * feat_dim // LANES
    top_pieces = top_block.reshape(group_width, piece_rows, LANES)
    summed = jnp.sum(swap(jnp.concatenate([found, top_pieces], axis=1), "sub"), axis=0)
    candidate_sq_distance = summed[:row_count]
    top_sums = summed[row_count:].reshape(top_rows, feat_dim)
    old_rows = lax.dynamic_slice_in_dim(old_top, device * top_rows, top_rows)
    new_rows = level_update(top_sums, top_totals, old_rows)
    new_block = spread(new_rows, "sub").reshape(group_width * top_rows, feat_dim)
    new_top = spread(new_block, "grp").reshape(top_count, feat_dim)
    return (new_fine, new_middle, new_top, candidate_sq_distance)


def solution(mesh):
    placed = (
        P(BOTH, None),
        P(BOTH),
        P(BOTH, None),
        P(BOTH, None),
        P(BOTH),
        P("grp", None),
        P("grp"),
        P(),
    )
    return jax.shard_map(
        per_device,
        mesh=mesh,
        in_specs=placed,
        out_specs=(P(BOTH, None), P("grp", None), P(), P(BOTH, None)),
        check_vma=False,
    )
```

```python
import functools

import jax
import jax.numpy as jnp
from jax import lax
from jax.experimental import pallas as pl
from jax.experimental.pallas import tpu as pltpu
from jax.sharding import PartitionSpec as P

CAP = 3
LANES = 128
SUBLANES = 8
LANE_BITS = 7
ID_BITS = 6
LOW_LANE = 8
COUNT_LANE = 16
FINE_STEP = 512
MIDDLE_STEP = 512
TOP_STEP = 512
EXACT = 256
SIDE = 4
MOST_SHARES = 16
BOTH = ("grp", "sub")


def level_update(totals, members, olds):
    return ((totals + olds.astype(jnp.float32)) / (members + 1.0)[:, None]).astype(jnp.bfloat16)


def swap(blocks, axes):
    return lax.all_to_all(blocks, axes, split_axis=0, concat_axis=0, tiled=True)


def spread(block, axes):
    copies = lax.axis_size(axes)
    return swap(jnp.broadcast_to(block[None], (copies,) + block.shape), axes)


def ring(count, apart, turn):
    pairs = []
    for i in range(count):
        place = i // apart % SIDE
        pairs.append((i, i + ((place + turn) % SIDE - place) * apart))
    return pairs


def dot(left, right):
    return jnp.dot(left, right, preferred_element_type=jnp.float32)


def hits(count, first, parents):
    rows = lax.broadcasted_iota(jnp.int32, (count, parents.shape[1]), 0) + first
    return rows == parents


def quick_table(rows, first, parents):
    pieces = []
    for begin in range(0, rows, EXACT):
        near = parents - (first + begin)
        near = jnp.where(jnp.logical_and(near >= 0, near < EXACT), near, -1)
        near = near.astype(jnp.float32).astype(jnp.bfloat16)
        ids = lax.broadcasted_iota(jnp.int32, (EXACT, parents.shape[1]), 0)
        ids = ids.astype(jnp.float32).astype(jnp.bfloat16)
        pieces.append(jnp.where(ids == near, jnp.bfloat16(1), jnp.bfloat16(0)))
    return jnp.concatenate(pieces, axis=0)


def column(row):
    count = row.shape[1]
    down = lax.broadcasted_iota(jnp.int32, (count, count), 0)
    along = lax.broadcasted_iota(jnp.int32, (count, count), 1)
    return jnp.sum(jnp.where(down == along, row, jnp.zeros_like(row)), axis=1, keepdims=True)


def small(numbers):
    return numbers.astype(jnp.float32).astype(jnp.bfloat16)


def send_kernel(
    share_ref,
    clusters_ref,
    points_ref,
    parents_ref,
    fine_parents_ref,
    candidates_ref,
    out_ref,
    wide_ref,
    counts_ref,
    *,
    fine_count,
):
    rows, feat_dim = points_ref.shape
    slots = out_ref.shape[0]
    slot_count = CAP + 1
    devices = slots // slot_count
    fine_bits = fine_count.bit_length() - 1
    clusters = clusters_ref[...]
    cluster_column = column(clusters)
    owners = lax.shift_right_logical(clusters, fine_bits)
    owner_column = lax.shift_right_logical(cluster_column, fine_bits)
    down = lax.broadcasted_iota(jnp.int32, (rows, rows), 0)
    along = lax.broadcasted_iota(jnp.int32, (rows, rows), 1)
    same = owner_column == owners
    ranks = jnp.sum(jnp.where(same & (down < along), 1, 0), axis=0, keepdims=True)
    rank_column = jnp.sum(jnp.where(same & (along < down), 1, 0), axis=1, keepdims=True)
    ids = jnp.bitwise_and(cluster_column, fine_count - 1)
    high = lax.shift_right_logical(ids, ID_BITS) + 1
    low = jnp.bitwise_and(ids, (1 << ID_BITS) - 1)
    lane = lax.broadcasted_iota(jnp.int32, (rows, feat_dim), 1)
    id_rows = jnp.where(lane == rank_column, high, jnp.where(lane == LOW_LANE + rank_column, low, 0))
    id_rows = id_rows.astype(jnp.float32).astype(jnp.bfloat16)
    share = share_ref[0]
    parents = parents_ref[:, pl.ds(pl.multiple_of(share * LANES, LANES), LANES)]
    top_bits = share_ref[2]
    table = hits(devices, 0, lax.shift_right_logical(parents, top_bits)).astype(jnp.bfloat16)
    within = jnp.bitwise_and(parents, lax.shift_left(jnp.int32(1), top_bits) - 1)
    spots = hits(feat_dim, 0, within + COUNT_LANE).astype(jnp.bfloat16)
    counts = lax.dot_general(
        table, spots, (((1,), (1,)), ((), ())), preferred_element_type=jnp.float32
    )
    counts = counts.astype(jnp.bfloat16)
    fine_parents = fine_parents_ref[...]
    shares = share_ref[1]
    share_of = jnp.bitwise_and(lax.shift_right_logical(fine_parents, LANE_BITS), shares - 1)
    table = hits(MOST_SHARES, 0, share_of).astype(jnp.bfloat16)
    spots = hits(LANES, 0, jnp.bitwise_and(fine_parents, LANES - 1)).astype(jnp.bfloat16)
    counts_ref[...] = lax.dot_general(
        table, spots, (((1,), (1,)), ((), ())), preferred_element_type=jnp.float32
    )
    place = jnp.bitwise_and(candidates_ref[...], fine_count - 1)
    chunk = lax.shift_right_logical(place, LANE_BITS)
    within = jnp.bitwise_and(place, LANES - 1)
    wide_ref[:, :feat_dim] = points_ref[...]
    wide_ref[:, feat_dim : feat_dim + LANES] = small(chunk)
    wide_ref[:, feat_dim + LANES : feat_dim + 2 * LANES] = small(within)
    every = lax.broadcasted_iota(jnp.int32, (1, devices), 1)
    sent = dot(hits(slots, 0, owners * slot_count + ranks).astype(jnp.bfloat16), points_ref[...])
    sent = sent + dot(hits(slots, 0, owners * slot_count + CAP).astype(jnp.bfloat16), id_rows)
    sent = sent + dot(hits(slots, 0, every * slot_count + CAP).astype(jnp.bfloat16), counts)
    out_ref[...] = sent.astype(jnp.bfloat16)


def outgoing(
    which, point_cluster, points, middle_parent, fine_parent, candidates, devices, fine_count
):
    rows, feat_dim = points.shape
    slots = devices * (CAP + 1)
    wide = feat_dim + 2 * LANES

    def whole(i, s):
        return (0, 0)

    return pl.pallas_call(
        functools.partial(send_kernel, fine_count=fine_count),
        out_shape=(
            jax.ShapeDtypeStruct((slots, feat_dim), jnp.bfloat16),
            jax.ShapeDtypeStruct((rows, wide), jnp.bfloat16),
            jax.ShapeDtypeStruct((MOST_SHARES, LANES), jnp.float32),
        ),
        grid_spec=pltpu.PrefetchScalarGridSpec(
            num_scalar_prefetch=1,
            grid=(1,),
            in_specs=[
                pl.BlockSpec((1, rows), whole),
                pl.BlockSpec((rows, feat_dim), whole),
                pl.BlockSpec((1, middle_parent.shape[0]), whole),
                pl.BlockSpec((1, fine_parent.shape[0]), whole),
                pl.BlockSpec(candidates.shape, whole),
            ],
            out_specs=[
                pl.BlockSpec((slots, feat_dim), whole),
                pl.BlockSpec((rows, wide), whole),
                pl.BlockSpec((MOST_SHARES, LANES), whole),
            ],
        ),
        compiler_params=pltpu.CompilerParams(vmem_limit_bytes=24 * 1024 * 1024),
        cost_estimate=pl.CostEstimate(
            flops=4 * slots * LANES * feat_dim, bytes_accessed=2 * 1024 * 1024, transcendentals=0
        ),
    )(
        which,
        point_cluster[None, :],
        points,
        middle_parent[None, :],
        fine_parent[None, :],
        candidates,
    )


def levels_kernel(
    share_ref,
    got_ref,
    ids_ref,
    old_fine_ref,
    parent_ref,
    members_ref,
    old_share_ref,
    top_parent_ref,
    fine_ref,
    middle_ref,
    top_ref,
    held,
    scaled,
    sent,
):
    step = pl.program_id(0)
    last = pl.num_programs(0) - 1
    fine_steps = held.shape[0] // FINE_STEP
    middle_steps = scaled.shape[0] // MIDDLE_STEP
    top_rows = top_ref.shape[0]
    store = pltpu.make_async_copy(held, fine_ref, sent)

    @pl.when(step < fine_steps)
    def _():
        first = pl.multiple_of(step * FINE_STEP, FINE_STEP)
        found = hits(FINE_STEP, first, ids_ref[...])
        members = jnp.sum(found.astype(jnp.float32), axis=1, keepdims=True)
        totals = dot(found.astype(jnp.bfloat16), got_ref[...])
        totals = totals + old_fine_ref[...].astype(jnp.float32)
        held[pl.ds(first, FINE_STEP), :] = (totals * (1.0 / (members + 1.0))).astype(jnp.bfloat16)

    @pl.when(step == fine_steps)
    def _():
        store.start()

    @pl.when(jnp.logical_and(step >= fine_steps, step < fine_steps + middle_steps))
    def _():
        first = pl.multiple_of((step - fine_steps) * MIDDLE_STEP, MIDDLE_STEP)
        part = dot(quick_table(MIDDLE_STEP, first, parent_ref[...]), held[...])
        middle_ref[...] = part.astype(jnp.bfloat16)
        block = (step - fine_steps) * (MIDDLE_STEP // LANES)
        rows = [members_ref[pl.ds(block + i, 1), :] for i in range(MIDDLE_STEP // LANES)]
        members = jnp.concatenate([column(row) for row in rows], axis=0)
        weighted = part * (1.0 / (members + 1.0))
        scaled[pl.ds(first, MIDDLE_STEP), :] = weighted.astype(jnp.bfloat16)

    @pl.when(step >= fine_steps + middle_steps)
    def _():
        first = (step - fine_steps - middle_steps) * top_rows
        olds = old_share_ref[...].astype(jnp.float32)
        members = column(members_ref[pl.ds(share_ref[0], 1), :])
        olds = (olds * (1.0 / (members + 1.0))).astype(jnp.bfloat16)
        own = pl.ds(pl.multiple_of(share_ref[0] * LANES, LANES), LANES)
        own_table = quick_table(top_rows, first, top_parent_ref[:, own])
        table = quick_table(top_rows, first, top_parent_ref[...])
        top_ref[...] = dot(table, scaled[...]) + dot(own_table, olds)

    @pl.when(step == last)
    def _():
        store.wait()


def levels(which, got, ids, old_fine, parents, members, old_middle, top_parents, top_count):
    fine_count, feat_dim = old_fine.shape
    middle_count = old_middle.shape[0]
    share_rows = members.shape[1]
    slots = got.shape[0]
    fine_steps = fine_count // FINE_STEP
    middle_steps = middle_count // MIDDLE_STEP
    top_steps = top_count // TOP_STEP

    def fine_at(i, s):
        return (jnp.minimum(i, fine_steps - 1), 0)

    def middle_at(i, s):
        return (jnp.clip(i - fine_steps, 0, middle_steps - 1), 0)

    def top_at(i, s):
        return (jnp.maximum(i - fine_steps - middle_steps, 0), 0)

    def whole(i, s):
        return (0, 0)

    flops = 2 * feat_dim * (fine_count * slots + middle_count * (fine_count + top_count))
    return pl.pallas_call(
        levels_kernel,
        out_shape=(
            jax.ShapeDtypeStruct((fine_count, feat_dim), jnp.bfloat16),
            jax.ShapeDtypeStruct((middle_count, feat_dim), jnp.bfloat16),
            jax.ShapeDtypeStruct((top_count, feat_dim), jnp.float32),
        ),
        grid_spec=pltpu.PrefetchScalarGridSpec(
            num_scalar_prefetch=1,
            grid=(fine_steps + middle_steps + top_steps,),
            in_specs=[
                pl.BlockSpec((slots, feat_dim), whole),
                pl.BlockSpec((1, slots), whole),
                pl.BlockSpec((FINE_STEP, feat_dim), fine_at),
                pl.BlockSpec((1, fine_count), whole),
                pl.BlockSpec(members.shape, whole),
                pl.BlockSpec((share_rows, feat_dim), lambda i, s: (s[0], 0)),
                pl.BlockSpec((1, middle_count), whole),
            ],
            out_specs=[
                pl.BlockSpec(memory_space=pl.ANY),
                pl.BlockSpec((MIDDLE_STEP, feat_dim), middle_at),
                pl.BlockSpec((TOP_STEP, feat_dim), top_at),
            ],
            scratch_shapes=[
                pltpu.VMEM((fine_count, feat_dim), jnp.bfloat16),
                pltpu.VMEM((middle_count, feat_dim), jnp.bfloat16),
                pltpu.SemaphoreType.DMA,
            ],
        ),
        compiler_params=pltpu.CompilerParams(vmem_limit_bytes=56 * 1024 * 1024),
        cost_estimate=pl.CostEstimate(
            flops=flops, bytes_accessed=18 * 1024 * 1024, transcendentals=0
        ),
    )(which, got, ids, old_fine, parents, members, old_middle, top_parents)


def distance_kernel(share_ref, rows_ref, fine_ref, norms_ref, out_ref):
    fine_count, feat_dim = fine_ref.shape
    rows = rows_ref.shape[0]
    block = rows_ref[:, :feat_dim]
    wide = block.astype(jnp.float32)
    point_norms = jnp.sum(wide * wide, axis=1, keepdims=True)
    cross = lax.dot_general(
        block, fine_ref[...], (((1,), (1,)), ((), ())), preferred_element_type=jnp.float32
    )
    places = rows_ref[:, feat_dim : feat_dim + 2 * LANES].astype(jnp.float32).astype(jnp.int32)
    chunk = places[:, :LANES]
    lane = places[:, LANES:]
    picked = jnp.zeros((rows, LANES), jnp.float32)
    for c in range(fine_count // LANES):
        here = slice(c * LANES, (c + 1) * LANES)
        scores = norms_ref[:, here] - 2.0 * cross[:, here]
        found = jnp.take_along_axis(scores, lane, axis=1)
        picked = jnp.where(chunk == c, found, picked)
    column = lax.broadcasted_iota(jnp.int32, (rows, LANES), 1)
    mine = jnp.bitwise_and(column, share_ref[1] - 1) == share_ref[0]
    total = jnp.maximum(picked + point_norms, 0.0) * (1.0 / feat_dim)
    total = jnp.where(mine, total, 0.0)
    per_block = rows // out_ref.shape[0]
    for block in range(out_ref.shape[0]):
        packed = jnp.zeros((SUBLANES, LANES), jnp.float32)
        for b in range(per_block // SUBLANES):
            first = block * per_block + b * SUBLANES
            shift = jnp.bitwise_and(b - share_ref[0] + LANES, LANES - 1)
            packed = packed + pltpu.roll(total[first : first + SUBLANES], shift, 1)
        out_ref[block] = packed


def candidate_parts(share, all_rows, old_fine, fine_norms, groups):
    row_count = all_rows.shape[0] // groups
    fine_count, feat_dim = old_fine.shape
    per_step = 2
    return pl.pallas_call(
        distance_kernel,
        out_shape=jax.ShapeDtypeStruct((groups, SUBLANES, LANES), jnp.float32),
        grid_spec=pltpu.PrefetchScalarGridSpec(
            num_scalar_prefetch=1,
            grid=(groups // per_step,),
            in_specs=[
                pl.BlockSpec((per_step * row_count, all_rows.shape[1]), lambda i, s: (i, 0)),
                pl.BlockSpec((fine_count, feat_dim), lambda i, s: (0, 0)),
                pl.BlockSpec((1, fine_count), lambda i, s: (0, 0)),
            ],
            out_specs=pl.BlockSpec((per_step, SUBLANES, LANES), lambda i, s: (i, 0, 0)),
        ),
        compiler_params=pltpu.CompilerParams(vmem_limit_bytes=40 * 1024 * 1024),
        cost_estimate=pl.CostEstimate(
            flops=2 * groups * row_count * fine_count * feat_dim,
            bytes_accessed=2 * (groups * row_count + fine_count) * feat_dim,
            transcendentals=0,
        ),
    )(share, all_rows, old_fine, fine_norms)


def place_kernel(at_ref, *refs):
    *pieces, out_ref = refs
    for i, piece in enumerate(pieces):
        row = pl.multiple_of(at_ref[i], piece.shape[0])
        out_ref[pl.ds(row, piece.shape[0]), :] = piece[...]


def all_blocks(block, total):
    places = lax.axis_size("grp")
    cores = places // SIDE
    onward = ring(places, cores, 1)
    backward = ring(places, cores, SIDE - 1)
    across = [(i, i ^ 1) for i in range(places)]
    rows = block.shape[0]
    half = rows // 2
    before = lax.ppermute(block, "grp", onward)
    after = lax.ppermute(block, "grp", backward)
    far_first = lax.ppermute(before[:half], "grp", onward)
    far_last = lax.ppermute(after[half:], "grp", backward)
    pieces = [block, before, after, far_first, far_last]
    pieces += [lax.ppermute(piece, "grp", across) for piece in pieces]
    me = lax.axis_index("grp")
    chip = me // cores
    starts = []
    for core in (me % cores, 1 - me % cores):
        for turn, shift in ((0, 0), (SIDE - 1, 0), (1, 0), (2, 0), (2, half)):
            starts.append(((chip + turn) % SIDE * cores + core) * rows + shift)
    return pl.pallas_call(
        place_kernel,
        out_shape=jax.ShapeDtypeStruct((total, block.shape[1]), block.dtype),
        grid_spec=pltpu.PrefetchScalarGridSpec(
            num_scalar_prefetch=1,
            grid=(1,),
            in_specs=[pl.BlockSpec(piece.shape, lambda i, at: (0, 0)) for piece in pieces],
            out_specs=pl.BlockSpec((total, block.shape[1]), lambda i, at: (0, 0)),
        ),
        compiler_params=pltpu.CompilerParams(vmem_limit_bytes=32 * 1024 * 1024),
        cost_estimate=pl.CostEstimate(flops=0, bytes_accessed=4 * 1024 * 1024, transcendentals=0),
    )(jnp.stack(starts).astype(jnp.int32), *pieces)


def per_device(
    points, point_cluster, candidates, old_fine, fine_parent, old_middle, middle_parent, old_top
):
    devices = lax.axis_size(BOTH)
    group_width = lax.axis_size("sub")
    share = lax.axis_index("sub")
    device = lax.axis_index(BOTH)
    row_count, feat_dim = points.shape
    fine_count = old_fine.shape[0]
    middle_count = old_middle.shape[0]
    top_count = old_top.shape[0]
    share_rows = middle_count // group_width
    top_rows = top_count // devices
    which = jnp.stack([share, jnp.int32(group_width), jnp.int32(top_rows.bit_length() - 1)])

    slot_count = CAP + 1
    send_rows, wide_rows, middle_members = outgoing(
        which,
        point_cluster,
        points,
        middle_parent,
        fine_parent,
        candidates,
        devices,
        fine_count,
    )
    got = swap(send_rows.reshape(devices, slot_count, feat_dim), BOTH)
    side = got[:, CAP, :LANES].astype(jnp.float32)
    got_high = side[:, :CAP].astype(jnp.int32)
    got_low = side[:, LOW_LANE : LOW_LANE + CAP].astype(jnp.int32)
    got_ids = jnp.where(got_high > 0, (got_high - 1) * (1 << ID_BITS) + got_low, -1)
    got_ids = jnp.pad(got_ids, ((0, 0), (0, 1)), constant_values=-1)
    top_totals = jnp.sum(side[:, COUNT_LANE : COUNT_LANE + top_rows], axis=0)

    all_rows = lax.all_gather(wide_rows, "sub", axis=0, tiled=True)
    for apart in (1, SIDE):
        around = [middle_members]
        for turn in range(1, SIDE):
            around.append(lax.ppermute(middle_members, "sub", ring(group_width, apart, turn)))
        middle_members = sum(around)

    middle_local = fine_parent - lax.axis_index("grp") * middle_count
    new_fine, middle_part, top_part = levels(
        which,
        got.reshape(devices * slot_count, feat_dim),
        got_ids.reshape(1, devices * slot_count),
        old_fine,
        middle_local[None, :],
        middle_members,
        old_middle,
        middle_parent[None, :],
        top_count,
    )

    parts = swap(middle_part.reshape(group_width, share_rows, feat_dim), "sub")
    wide_fine = old_fine.astype(jnp.float32)
    fine_norms = jnp.sum(wide_fine * wide_fine, axis=1)[None, :]
    found = candidate_parts(which, all_rows, old_fine, fine_norms, group_width)
    parts, found = lax.optimization_barrier((parts, found))
    share_totals = lax.dynamic_slice_in_dim(middle_members, share, 1).reshape(share_rows)
    old_share = lax.dynamic_slice_in_dim(old_middle, share * share_rows, share_rows)
    new_share = level_update(jnp.sum(parts.astype(jnp.float32), axis=0), share_totals, old_share)
    new_middle = lax.all_gather(new_share, "sub", axis=0, tiled=True)

    top_block = lax.psum_scatter(top_part, "grp", scatter_dimension=0, tiled=True)
    top_pieces = top_block.reshape(group_width, top_rows, feat_dim)
    returned = swap(jnp.concatenate([top_pieces, found], axis=2), "sub")
    top_sums = jnp.sum(returned[:, :, :feat_dim], axis=0)
    packed = returned[:, :, feat_dim:].reshape(group_width, SUBLANES, -1, group_width)
    packed = packed[..., : row_count // SUBLANES]
    candidate_sq_distance = packed.transpose(3, 1, 2, 0).reshape(row_count, -1)
    old_rows = lax.dynamic_slice_in_dim(old_top, device * top_rows, top_rows)
    new_rows = level_update(top_sums, top_totals, old_rows)
    new_block = spread(new_rows, "sub").reshape(group_width * top_rows, feat_dim)
    new_top = all_blocks(new_block, top_count)
    return (new_fine, new_middle, new_top, candidate_sq_distance)


def solution(mesh):
    placed = (
        P(BOTH, None),
        P(BOTH),
        P(BOTH, None),
        P(BOTH, None),
        P(BOTH),
        P("grp", None),
        P("grp"),
        P(),
    )
    return jax.shard_map(
        per_device,
        mesh=mesh,
        in_specs=placed,
        out_specs=(P(BOTH, None), P("grp", None), P(), P(BOTH, None)),
        check_vma=False,
    )
```

```python
import functools

import jax
import jax.numpy as jnp
from jax import lax
from jax.experimental import pallas as pl
from jax.experimental.pallas import tpu as pltpu
from jax.sharding import PartitionSpec as P

CAP = 3
LANES = 128
SUBLANES = 8
LANE_BITS = 7
ID_BITS = 6
LOW_LANE = 8
COUNT_LANE = 16
FINE_STEP = 512
MIDDLE_STEP = 512
TOP_STEP = 512
LEFT_STEP = 1024
EXACT = 256
SIDE = 4
MOST_SHARES = 16
LONG = 1_000_000_000_000
BOTH = ("grp", "sub")


def level_update(totals, members, olds):
    return ((totals + olds.astype(jnp.float32)) / (members + 1.0)[:, None]).astype(jnp.bfloat16)


def swap(blocks, axes):
    return lax.all_to_all(blocks, axes, split_axis=0, concat_axis=0, tiled=True)


def spread(block, axes):
    copies = lax.axis_size(axes)
    return swap(jnp.broadcast_to(block[None], (copies,) + block.shape), axes)


def ring(count, apart, turn):
    pairs = []
    for i in range(count):
        place = i // apart % SIDE
        pairs.append((i, i + ((place + turn) % SIDE - place) * apart))
    return pairs


def dot(left, right):
    return jnp.dot(left, right, preferred_element_type=jnp.float32)


def hits(count, first, parents):
    rows = lax.broadcasted_iota(jnp.int32, (count, parents.shape[1]), 0) + first
    return rows == parents


def quick_table(rows, first, parents):
    pieces = []
    for begin in range(0, rows, EXACT):
        near = parents - (first + begin)
        near = jnp.where(jnp.logical_and(near >= 0, near < EXACT), near, -1)
        near = near.astype(jnp.float32).astype(jnp.bfloat16)
        ids = lax.broadcasted_iota(jnp.int32, (EXACT, parents.shape[1]), 0)
        ids = ids.astype(jnp.float32).astype(jnp.bfloat16)
        pieces.append(jnp.where(ids == near, jnp.bfloat16(1), jnp.bfloat16(0)))
    return jnp.concatenate(pieces, axis=0)


def column(row):
    count = row.shape[1]
    down = lax.broadcasted_iota(jnp.int32, (count, count), 0)
    along = lax.broadcasted_iota(jnp.int32, (count, count), 1)
    return jnp.sum(jnp.where(down == along, row, jnp.zeros_like(row)), axis=1, keepdims=True)


def small(numbers):
    return numbers.astype(jnp.float32).astype(jnp.bfloat16)


def send_kernel(
    share_ref,
    clusters_ref,
    points_ref,
    parents_ref,
    fine_parents_ref,
    candidates_ref,
    out_ref,
    wide_ref,
    counts_ref,
    *,
    fine_count,
):
    rows, feat_dim = points_ref.shape
    slots = out_ref.shape[0]
    slot_count = CAP + 1
    devices = slots // slot_count
    fine_bits = fine_count.bit_length() - 1
    clusters = clusters_ref[...]
    cluster_column = column(clusters)
    owners = lax.shift_right_logical(clusters, fine_bits)
    owner_column = lax.shift_right_logical(cluster_column, fine_bits)
    down = lax.broadcasted_iota(jnp.int32, (rows, rows), 0)
    along = lax.broadcasted_iota(jnp.int32, (rows, rows), 1)
    same = owner_column == owners
    ranks = jnp.sum(jnp.where(same & (down < along), 1, 0), axis=0, keepdims=True)
    rank_column = jnp.sum(jnp.where(same & (along < down), 1, 0), axis=1, keepdims=True)
    ids = jnp.bitwise_and(cluster_column, fine_count - 1)
    high = lax.shift_right_logical(ids, ID_BITS) + 1
    low = jnp.bitwise_and(ids, (1 << ID_BITS) - 1)
    lane = lax.broadcasted_iota(jnp.int32, (rows, feat_dim), 1)
    id_rows = jnp.where(lane == rank_column, high, jnp.where(lane == LOW_LANE + rank_column, low, 0))
    id_rows = id_rows.astype(jnp.float32).astype(jnp.bfloat16)
    share = share_ref[0]
    parents = parents_ref[:, pl.ds(pl.multiple_of(share * LANES, LANES), LANES)]
    top_bits = share_ref[2]
    table = hits(devices, 0, lax.shift_right_logical(parents, top_bits)).astype(jnp.bfloat16)
    within = jnp.bitwise_and(parents, lax.shift_left(jnp.int32(1), top_bits) - 1)
    spots = hits(feat_dim, 0, within + COUNT_LANE).astype(jnp.bfloat16)
    counts = lax.dot_general(
        table, spots, (((1,), (1,)), ((), ())), preferred_element_type=jnp.float32
    )
    counts = counts.astype(jnp.bfloat16)
    fine_parents = fine_parents_ref[...]
    shares = share_ref[1]
    share_of = jnp.bitwise_and(lax.shift_right_logical(fine_parents, LANE_BITS), shares - 1)
    table = hits(MOST_SHARES, 0, share_of).astype(jnp.bfloat16)
    spots = hits(LANES, 0, jnp.bitwise_and(fine_parents, LANES - 1)).astype(jnp.bfloat16)
    counts_ref[...] = lax.dot_general(
        table, spots, (((1,), (1,)), ((), ())), preferred_element_type=jnp.float32
    )
    place = jnp.bitwise_and(candidates_ref[...], fine_count - 1)
    chunk = lax.shift_right_logical(place, LANE_BITS)
    within = jnp.bitwise_and(place, LANES - 1)
    wide_ref[:, :feat_dim] = points_ref[...]
    wide_ref[:, feat_dim : feat_dim + LANES] = small(chunk)
    wide_ref[:, feat_dim + LANES : feat_dim + 2 * LANES] = small(within)
    every = lax.broadcasted_iota(jnp.int32, (1, devices), 1)
    sent = dot(hits(slots, 0, owners * slot_count + ranks).astype(jnp.bfloat16), points_ref[...])
    sent = sent + dot(hits(slots, 0, owners * slot_count + CAP).astype(jnp.bfloat16), id_rows)
    sent = sent + dot(hits(slots, 0, every * slot_count + CAP).astype(jnp.bfloat16), counts)
    out_ref[...] = sent.astype(jnp.bfloat16)


def outgoing(
    which, point_cluster, points, middle_parent, fine_parent, candidates, devices, fine_count
):
    rows, feat_dim = points.shape
    slots = devices * (CAP + 1)
    wide = feat_dim + 2 * LANES

    def whole(i, s):
        return (0, 0)

    return pl.pallas_call(
        functools.partial(send_kernel, fine_count=fine_count),
        out_shape=(
            jax.ShapeDtypeStruct((slots, feat_dim), jnp.bfloat16),
            jax.ShapeDtypeStruct((rows, wide), jnp.bfloat16),
            jax.ShapeDtypeStruct((MOST_SHARES, LANES), jnp.float32),
        ),
        grid_spec=pltpu.PrefetchScalarGridSpec(
            num_scalar_prefetch=1,
            grid=(1,),
            in_specs=[
                pl.BlockSpec((1, rows), whole),
                pl.BlockSpec((rows, feat_dim), whole),
                pl.BlockSpec((1, middle_parent.shape[0]), whole),
                pl.BlockSpec((1, fine_parent.shape[0]), whole),
                pl.BlockSpec(candidates.shape, whole),
            ],
            out_specs=[
                pl.BlockSpec((slots, feat_dim), whole),
                pl.BlockSpec((rows, wide), whole),
                pl.BlockSpec((MOST_SHARES, LANES), whole),
            ],
        ),
        compiler_params=pltpu.CompilerParams(vmem_limit_bytes=24 * 1024 * 1024),
        cost_estimate=pl.CostEstimate(
            flops=4 * slots * LANES * feat_dim, bytes_accessed=2 * 1024 * 1024, transcendentals=0
        ),
    )(
        which,
        point_cluster[None, :],
        points,
        middle_parent[None, :],
        fine_parent[None, :],
        candidates,
    )


def fine_step(step, got_ref, ids_ref, old_fine_ref, held):
    first = pl.multiple_of(step * FINE_STEP, FINE_STEP)
    found = hits(FINE_STEP, first, ids_ref[...])
    members = jnp.sum(found.astype(jnp.float32), axis=1, keepdims=True)
    totals = dot(found.astype(jnp.bfloat16), got_ref[...])
    totals = totals + old_fine_ref[...].astype(jnp.float32)
    held[pl.ds(first, FINE_STEP), :] = (totals * (1.0 / (members + 1.0))).astype(jnp.bfloat16)


def left_kernel(got_ref, ids_ref, old_fine_ref, parent_ref, fine_ref, middle_ref, held, sent):
    step = pl.program_id(0)
    fine_steps = held.shape[0] // FINE_STEP
    store = pltpu.make_async_copy(held, fine_ref.at[:, : held.shape[1]], sent)

    @pl.when(step < fine_steps)
    def _():
        fine_step(step, got_ref, ids_ref, old_fine_ref, held)

    @pl.when(step == fine_steps)
    def _():
        store.start()

    @pl.when(step >= fine_steps)
    def _():
        first = (step - fine_steps) * LEFT_STEP
        table = quick_table(LEFT_STEP, first, parent_ref[...])
        middle_ref[...] = dot(table, held[...]).astype(jnp.bfloat16)

    @pl.when(step == pl.num_programs(0) - 1)
    def _():
        store.wait()


def left_levels(got, ids, old_fine, parents, middle_count):
    fine_count, feat_dim = old_fine.shape
    half = feat_dim // 2
    slots = got.shape[0]
    fine_steps = fine_count // FINE_STEP

    def whole(i):
        return (0, 0)

    return pl.pallas_call(
        left_kernel,
        out_shape=(
            jax.ShapeDtypeStruct((fine_count, feat_dim), jnp.bfloat16),
            jax.ShapeDtypeStruct((middle_count, half), jnp.bfloat16),
        ),
        grid=(fine_steps + middle_count // LEFT_STEP,),
        in_specs=[
            pl.BlockSpec((slots, half), whole),
            pl.BlockSpec((1, slots), whole),
            pl.BlockSpec((FINE_STEP, half), lambda i: (jnp.minimum(i, fine_steps - 1), 0)),
            pl.BlockSpec((1, fine_count), whole),
        ],
        out_specs=[
            pl.BlockSpec(memory_space=pl.ANY),
            pl.BlockSpec((LEFT_STEP, half), lambda i: (jnp.maximum(i - fine_steps, 0), 0)),
        ],
        scratch_shapes=[
            pltpu.VMEM((fine_count, half), jnp.bfloat16),
            pltpu.SemaphoreType.DMA,
        ],
        compiler_params=pltpu.CompilerParams(vmem_limit_bytes=56 * 1024 * 1024),
        cost_estimate=pl.CostEstimate(
            flops=2 * half * fine_count * (slots + middle_count),
            bytes_accessed=8 * 1024 * 1024,
            transcendentals=0,
        ),
    )(got, ids, old_fine, parents)


def right_kernel(
    share_ref,
    got_ref,
    ids_ref,
    old_fine_ref,
    parent_ref,
    members_ref,
    old_share_ref,
    top_parent_ref,
    left_ref,
    kept_ref,
    fine_ref,
    middle_ref,
    top_ref,
    held,
    scaled,
    sent,
):
    del kept_ref
    step = pl.program_id(0)
    fine_steps = held.shape[0] // FINE_STEP
    middle_steps = scaled.shape[0] // MIDDLE_STEP
    top_rows = top_ref.shape[0]
    half = held.shape[1]
    store = pltpu.make_async_copy(held, fine_ref.at[:, half:], sent)

    @pl.when(step < fine_steps)
    def _():
        fine_step(step, got_ref, ids_ref, old_fine_ref, held)

    @pl.when(step == fine_steps)
    def _():
        store.start()

    @pl.when(jnp.logical_and(step >= fine_steps, step < fine_steps + middle_steps))
    def _():
        first = pl.multiple_of((step - fine_steps) * MIDDLE_STEP, MIDDLE_STEP)
        part = dot(quick_table(MIDDLE_STEP, first, parent_ref[...]), held[...])
        middle_ref[...] = part.astype(jnp.bfloat16)
        block = (step - fine_steps) * (MIDDLE_STEP // LANES)
        rows = [members_ref[pl.ds(block + i, 1), :] for i in range(MIDDLE_STEP // LANES)]
        weights = 1.0 / (jnp.concatenate([column(row) for row in rows], axis=0) + 1.0)
        left = left_ref[...].astype(jnp.float32) * weights
        scaled[pl.ds(first, MIDDLE_STEP), :half] = left.astype(jnp.bfloat16)
        scaled[pl.ds(first, MIDDLE_STEP), half:] = (part * weights).astype(jnp.bfloat16)

    @pl.when(step >= fine_steps + middle_steps)
    def _():
        first = (step - fine_steps - middle_steps) * top_rows
        olds = old_share_ref[...].astype(jnp.float32)
        members = column(members_ref[pl.ds(share_ref[0], 1), :])
        olds = (olds * (1.0 / (members + 1.0))).astype(jnp.bfloat16)
        own = pl.ds(pl.multiple_of(share_ref[0] * LANES, LANES), LANES)
        own_table = quick_table(top_rows, first, top_parent_ref[:, own])
        table = quick_table(top_rows, first, top_parent_ref[...])
        top_ref[...] = dot(table, scaled[...]) + dot(own_table, olds)

    @pl.when(step == pl.num_programs(0) - 1)
    def _():
        store.wait()


def right_levels(
    which, got, ids, old_fine, parents, members, old_middle, top_parents, left, kept, top_count
):
    fine_count, feat_dim = old_fine.shape
    half = feat_dim // 2
    middle_count = old_middle.shape[0]
    share_rows = members.shape[1]
    slots = got.shape[0]
    fine_steps = fine_count // FINE_STEP
    middle_steps = middle_count // MIDDLE_STEP
    top_steps = top_count // TOP_STEP

    def fine_at(i, s):
        return (jnp.minimum(i, fine_steps - 1), 1)

    def middle_at(i, s):
        return (jnp.clip(i - fine_steps, 0, middle_steps - 1), 0)

    def top_at(i, s):
        return (jnp.maximum(i - fine_steps - middle_steps, 0), 0)

    def whole(i, s):
        return (0, 0)

    flops = 2 * half * (fine_count * slots + middle_count * (fine_count + 2 * top_count))
    return pl.pallas_call(
        right_kernel,
        out_shape=(
            jax.ShapeDtypeStruct((fine_count, feat_dim), jnp.bfloat16),
            jax.ShapeDtypeStruct((middle_count, half), jnp.bfloat16),
            jax.ShapeDtypeStruct((top_count, feat_dim), jnp.float32),
        ),
        grid_spec=pltpu.PrefetchScalarGridSpec(
            num_scalar_prefetch=1,
            grid=(fine_steps + middle_steps + top_steps,),
            in_specs=[
                pl.BlockSpec((slots, half), lambda i, s: (0, 1)),
                pl.BlockSpec((1, slots), whole),
                pl.BlockSpec((FINE_STEP, half), fine_at),
                pl.BlockSpec((1, fine_count), whole),
                pl.BlockSpec(members.shape, whole),
                pl.BlockSpec((share_rows, feat_dim), lambda i, s: (s[0], 0)),
                pl.BlockSpec((1, middle_count), whole),
                pl.BlockSpec((MIDDLE_STEP, half), middle_at),
                pl.BlockSpec(memory_space=pl.ANY),
            ],
            out_specs=[
                pl.BlockSpec(memory_space=pl.ANY),
                pl.BlockSpec((MIDDLE_STEP, half), middle_at),
                pl.BlockSpec((TOP_STEP, feat_dim), top_at),
            ],
            scratch_shapes=[
                pltpu.VMEM((fine_count, half), jnp.bfloat16),
                pltpu.VMEM((middle_count, feat_dim), jnp.bfloat16),
                pltpu.SemaphoreType.DMA,
            ],
        ),
        input_output_aliases={9: 0},
        compiler_params=pltpu.CompilerParams(vmem_limit_bytes=56 * 1024 * 1024),
        cost_estimate=pl.CostEstimate(
            flops=flops, bytes_accessed=14 * 1024 * 1024, transcendentals=0
        ),
    )(which, got, ids, old_fine, parents, members, old_middle, top_parents, left, kept)


def distance_kernel(share_ref, rows_ref, fine_ref, norms_ref, out_ref):
    fine_count, feat_dim = fine_ref.shape
    rows = rows_ref.shape[0]
    block = rows_ref[:, :feat_dim]
    wide = block.astype(jnp.float32)
    point_norms = jnp.sum(wide * wide, axis=1, keepdims=True)
    cross = lax.dot_general(
        block, fine_ref[...], (((1,), (1,)), ((), ())), preferred_element_type=jnp.float32
    )
    places = rows_ref[:, feat_dim : feat_dim + 2 * LANES].astype(jnp.float32).astype(jnp.int32)
    chunk = places[:, :LANES]
    lane = places[:, LANES:]
    picked = jnp.zeros((rows, LANES), jnp.float32)
    for c in range(fine_count // LANES):
        here = slice(c * LANES, (c + 1) * LANES)
        scores = norms_ref[:, here] - 2.0 * cross[:, here]
        found = jnp.take_along_axis(scores, lane, axis=1)
        picked = jnp.where(chunk == c, found, picked)
    column = lax.broadcasted_iota(jnp.int32, (rows, LANES), 1)
    mine = jnp.bitwise_and(column, share_ref[1] - 1) == share_ref[0]
    total = jnp.maximum(picked + point_norms, 0.0) * (1.0 / feat_dim)
    total = jnp.where(mine, total, 0.0)
    per_block = rows // out_ref.shape[0]
    for block in range(out_ref.shape[0]):
        packed = jnp.zeros((SUBLANES, LANES), jnp.float32)
        for b in range(per_block // SUBLANES):
            first = block * per_block + b * SUBLANES
            shift = jnp.bitwise_and(b - share_ref[0] + LANES, LANES - 1)
            packed = packed + pltpu.roll(total[first : first + SUBLANES], shift, 1)
        out_ref[block] = packed


def candidate_parts(share, all_rows, old_fine, fine_norms, groups):
    row_count = all_rows.shape[0] // groups
    fine_count, feat_dim = old_fine.shape
    per_step = 2
    return pl.pallas_call(
        distance_kernel,
        out_shape=jax.ShapeDtypeStruct((groups, SUBLANES, LANES), jnp.float32),
        grid_spec=pltpu.PrefetchScalarGridSpec(
            num_scalar_prefetch=1,
            grid=(groups // per_step,),
            in_specs=[
                pl.BlockSpec((per_step * row_count, all_rows.shape[1]), lambda i, s: (i, 0)),
                pl.BlockSpec((fine_count, feat_dim), lambda i, s: (0, 0)),
                pl.BlockSpec((1, fine_count), lambda i, s: (0, 0)),
            ],
            out_specs=pl.BlockSpec((per_step, SUBLANES, LANES), lambda i, s: (i, 0, 0)),
        ),
        compiler_params=pltpu.CompilerParams(vmem_limit_bytes=40 * 1024 * 1024),
        cost_estimate=pl.CostEstimate(
            flops=LONG,
            bytes_accessed=2 * (groups * row_count + fine_count) * feat_dim,
            transcendentals=0,
        ),
    )(share, all_rows, old_fine, fine_norms)


def place_kernel(at_ref, *refs):
    *pieces, out_ref = refs
    for i, piece in enumerate(pieces):
        row = pl.multiple_of(at_ref[i], piece.shape[0])
        out_ref[pl.ds(row, piece.shape[0]), :] = piece[...]


def all_blocks(block, total):
    places = lax.axis_size("grp")
    cores = places // SIDE
    onward = ring(places, cores, 1)
    backward = ring(places, cores, SIDE - 1)
    across = [(i, i ^ 1) for i in range(places)]
    rows = block.shape[0]
    half = rows // 2
    before = lax.ppermute(block, "grp", onward)
    after = lax.ppermute(block, "grp", backward)
    far_first = lax.ppermute(before[:half], "grp", onward)
    far_last = lax.ppermute(after[half:], "grp", backward)
    pieces = [block, before, after, far_first, far_last]
    pieces += [lax.ppermute(piece, "grp", across) for piece in pieces]
    me = lax.axis_index("grp")
    chip = me // cores
    starts = []
    for core in (me % cores, 1 - me % cores):
        for turn, shift in ((0, 0), (SIDE - 1, 0), (1, 0), (2, 0), (2, half)):
            starts.append(((chip + turn) % SIDE * cores + core) * rows + shift)
    return pl.pallas_call(
        place_kernel,
        out_shape=jax.ShapeDtypeStruct((total, block.shape[1]), block.dtype),
        grid_spec=pltpu.PrefetchScalarGridSpec(
            num_scalar_prefetch=1,
            grid=(1,),
            in_specs=[pl.BlockSpec(piece.shape, lambda i, at: (0, 0)) for piece in pieces],
            out_specs=pl.BlockSpec((total, block.shape[1]), lambda i, at: (0, 0)),
        ),
        compiler_params=pltpu.CompilerParams(vmem_limit_bytes=32 * 1024 * 1024),
        cost_estimate=pl.CostEstimate(flops=0, bytes_accessed=4 * 1024 * 1024, transcendentals=0),
    )(jnp.stack(starts).astype(jnp.int32), *pieces)


def per_device(
    points, point_cluster, candidates, old_fine, fine_parent, old_middle, middle_parent, old_top
):
    devices = lax.axis_size(BOTH)
    group_width = lax.axis_size("sub")
    share = lax.axis_index("sub")
    device = lax.axis_index(BOTH)
    row_count, feat_dim = points.shape
    fine_count = old_fine.shape[0]
    middle_count = old_middle.shape[0]
    top_count = old_top.shape[0]
    share_rows = middle_count // group_width
    top_rows = top_count // devices
    which = jnp.stack([share, jnp.int32(group_width), jnp.int32(top_rows.bit_length() - 1)])

    slot_count = CAP + 1
    send_rows, wide_rows, middle_members = outgoing(
        which,
        point_cluster,
        points,
        middle_parent,
        fine_parent,
        candidates,
        devices,
        fine_count,
    )
    got = swap(send_rows.reshape(devices, slot_count, feat_dim), BOTH)
    side = got[:, CAP, :LANES].astype(jnp.float32)
    got_high = side[:, :CAP].astype(jnp.int32)
    got_low = side[:, LOW_LANE : LOW_LANE + CAP].astype(jnp.int32)
    got_ids = jnp.where(got_high > 0, (got_high - 1) * (1 << ID_BITS) + got_low, -1)
    got_ids = jnp.pad(got_ids, ((0, 0), (0, 1)), constant_values=-1)
    top_totals = jnp.sum(side[:, COUNT_LANE : COUNT_LANE + top_rows], axis=0)

    all_rows = lax.all_gather(wide_rows, "sub", axis=0, tiled=True)
    for apart in (1, SIDE):
        around = [middle_members]
        for turn in range(1, SIDE):
            around.append(lax.ppermute(middle_members, "sub", ring(group_width, apart, turn)))
        middle_members = sum(around)

    middle_local = fine_parent - lax.axis_index("grp") * middle_count
    got = got.reshape(devices * slot_count, feat_dim)
    got_ids = got_ids.reshape(1, devices * slot_count)
    got_ids, middle_members = lax.optimization_barrier((got_ids, middle_members))
    parents = middle_local[None, :]
    half_fine, left = left_levels(got, got_ids, old_fine, parents, middle_count)
    new_fine, right, top_part = right_levels(
        which,
        got,
        got_ids,
        old_fine,
        parents,
        middle_members,
        old_middle,
        middle_parent[None, :],
        left,
        half_fine,
        top_count,
    )

    shares = (group_width, share_rows, feat_dim // 2)
    left = swap(left.reshape(shares), "sub")
    right, left = lax.optimization_barrier((right, left))
    right = swap(right.reshape(shares), "sub")
    wide_fine = old_fine.astype(jnp.float32)
    fine_norms = jnp.sum(wide_fine * wide_fine, axis=1)[None, :]
    found = candidate_parts(which, all_rows, old_fine, fine_norms, group_width)
    left, right, found = lax.optimization_barrier((left, right, found))
    share_totals = lax.dynamic_slice_in_dim(middle_members, share, 1).reshape(share_rows)
    old_share = lax.dynamic_slice_in_dim(old_middle, share * share_rows, share_rows)
    sums = [jnp.sum(parts.astype(jnp.float32), axis=0) for parts in (left, right)]
    new_share = level_update(jnp.concatenate(sums, axis=1), share_totals, old_share)
    new_middle = lax.all_gather(new_share, "sub", axis=0, tiled=True)

    top_block = lax.psum_scatter(top_part, "grp", scatter_dimension=0, tiled=True)
    top_pieces = top_block.reshape(group_width, top_rows, feat_dim)
    returned = swap(jnp.concatenate([top_pieces, found], axis=2), "sub")
    top_sums = jnp.sum(returned[:, :, :feat_dim], axis=0)
    packed = returned[:, :, feat_dim:].reshape(group_width, SUBLANES, -1, group_width)
    packed = packed[..., : row_count // SUBLANES]
    candidate_sq_distance = packed.transpose(3, 1, 2, 0).reshape(row_count, -1)
    old_rows = lax.dynamic_slice_in_dim(old_top, device * top_rows, top_rows)
    new_rows = level_update(top_sums, top_totals, old_rows)
    new_block = spread(new_rows, "sub").reshape(group_width * top_rows, feat_dim)
    new_top = all_blocks(new_block, top_count)
    return (new_fine, new_middle, new_top, candidate_sq_distance)


def solution(mesh):
    placed = (
        P(BOTH, None),
        P(BOTH),
        P(BOTH, None),
        P(BOTH, None),
        P(BOTH),
        P("grp", None),
        P("grp"),
        P(),
    )
    return jax.shard_map(
        per_device,
        mesh=mesh,
        in_specs=placed,
        out_specs=(P(BOTH, None), P("grp", None), P(), P(BOTH, None)),
        check_vma=False,
    )
```

```python
import functools

import jax
import jax.numpy as jnp
from jax import lax
from jax.experimental import pallas as pl
from jax.experimental.pallas import tpu as pltpu
from jax.sharding import PartitionSpec as P

CAP = 3
LANES = 128
SUBLANES = 8
LANE_BITS = 7
ID_BITS = 6
LOW_LANE = 8
COUNT_LANE = 16
FINE_STEP = 1024
MIDDLE_STEP = 512
TOP_STEP = 512
LEFT_STEP = 1024
EXACT = 256
SIDE = 4
MOST_SHARES = 16
COPY_CHUNKS = 8
LEFT_PARTS = 4
LONG = 1_000_000_000_000
BOTH = ("grp", "sub")


def level_update(totals, members, olds):
    return ((totals + olds.astype(jnp.float32)) / (members + 1.0)[:, None]).astype(jnp.bfloat16)


def swap(blocks, axes):
    return lax.all_to_all(blocks, axes, split_axis=0, concat_axis=0, tiled=True)


def spread(block, axes):
    copies = lax.axis_size(axes)
    return swap(jnp.broadcast_to(block[None], (copies,) + block.shape), axes)


def copy_kernel(in_ref, out_ref, held, got, sent):
    chunk = in_ref.shape[0] // COPY_CHUNKS
    loads, stores = [], []
    for i in range(COPY_CHUNKS):
        here = pl.ds(i * chunk, chunk)
        loads.append(pltpu.make_async_copy(in_ref.at[here], held.at[here], got.at[i]))
        stores.append(pltpu.make_async_copy(held.at[here], out_ref.at[here], sent.at[i]))
    for load in loads:
        load.start()
    for load, store in zip(loads, stores):
        load.wait()
        store.start()
    for store in stores:
        store.wait()


def copied(array):
    return pl.pallas_call(
        copy_kernel,
        out_shape=jax.ShapeDtypeStruct(array.shape, array.dtype),
        in_specs=[pl.BlockSpec(memory_space=pl.ANY)],
        out_specs=pl.BlockSpec(memory_space=pl.ANY),
        scratch_shapes=[
            pltpu.VMEM(array.shape, array.dtype),
            pltpu.SemaphoreType.DMA((COPY_CHUNKS,)),
            pltpu.SemaphoreType.DMA((COPY_CHUNKS,)),
        ],
        compiler_params=pltpu.CompilerParams(vmem_limit_bytes=60 * 1024 * 1024),
        cost_estimate=pl.CostEstimate(flops=0, bytes_accessed=4 * array.size, transcendentals=0),
    )(array)


def ring(count, apart, turn):
    pairs = []
    for i in range(count):
        place = i // apart % SIDE
        pairs.append((i, i + ((place + turn) % SIDE - place) * apart))
    return pairs


def dot(left, right):
    return jnp.dot(left, right, preferred_element_type=jnp.float32)


def hits(count, first, parents):
    rows = lax.broadcasted_iota(jnp.int32, (count, parents.shape[1]), 0) + first
    return rows == parents


def quick_table(rows, first, parents):
    pieces = []
    for begin in range(0, rows, EXACT):
        near = parents - (first + begin)
        near = jnp.where(jnp.logical_and(near >= 0, near < EXACT), near, -1)
        near = near.astype(jnp.float32).astype(jnp.bfloat16)
        ids = lax.broadcasted_iota(jnp.int32, (EXACT, parents.shape[1]), 0)
        ids = ids.astype(jnp.float32).astype(jnp.bfloat16)
        pieces.append(jnp.where(ids == near, jnp.bfloat16(1), jnp.bfloat16(0)))
    return jnp.concatenate(pieces, axis=0)


def column(row):
    count = row.shape[1]
    down = lax.broadcasted_iota(jnp.int32, (count, count), 0)
    along = lax.broadcasted_iota(jnp.int32, (count, count), 1)
    return jnp.sum(jnp.where(down == along, row, jnp.zeros_like(row)), axis=1, keepdims=True)


def small(numbers):
    return numbers.astype(jnp.float32).astype(jnp.bfloat16)


def send_kernel(
    share_ref,
    clusters_ref,
    points_ref,
    parents_ref,
    fine_parents_ref,
    candidates_ref,
    out_ref,
    wide_ref,
    counts_ref,
    *,
    fine_count,
):
    rows, feat_dim = points_ref.shape
    slots = out_ref.shape[0]
    slot_count = CAP + 1
    devices = slots // slot_count
    fine_bits = fine_count.bit_length() - 1
    clusters = clusters_ref[...]
    cluster_column = column(clusters)
    owners = lax.shift_right_logical(clusters, fine_bits)
    owner_column = lax.shift_right_logical(cluster_column, fine_bits)
    down = lax.broadcasted_iota(jnp.int32, (rows, rows), 0)
    along = lax.broadcasted_iota(jnp.int32, (rows, rows), 1)
    same = owner_column == owners
    ranks = jnp.sum(jnp.where(same & (down < along), 1, 0), axis=0, keepdims=True)
    rank_column = jnp.sum(jnp.where(same & (along < down), 1, 0), axis=1, keepdims=True)
    ids = jnp.bitwise_and(cluster_column, fine_count - 1)
    high = lax.shift_right_logical(ids, ID_BITS) + 1
    low = jnp.bitwise_and(ids, (1 << ID_BITS) - 1)
    lane = lax.broadcasted_iota(jnp.int32, (rows, feat_dim), 1)
    id_rows = jnp.where(lane == rank_column, high, jnp.where(lane == LOW_LANE + rank_column, low, 0))
    id_rows = id_rows.astype(jnp.float32).astype(jnp.bfloat16)
    share = share_ref[0]
    parents = parents_ref[:, pl.ds(pl.multiple_of(share * LANES, LANES), LANES)]
    top_bits = share_ref[2]
    table = hits(devices, 0, lax.shift_right_logical(parents, top_bits)).astype(jnp.bfloat16)
    within = jnp.bitwise_and(parents, lax.shift_left(jnp.int32(1), top_bits) - 1)
    spots = hits(feat_dim, 0, within + COUNT_LANE).astype(jnp.bfloat16)
    counts = lax.dot_general(
        table, spots, (((1,), (1,)), ((), ())), preferred_element_type=jnp.float32
    )
    counts = counts.astype(jnp.bfloat16)
    fine_parents = fine_parents_ref[...]
    shares = share_ref[1]
    share_of = jnp.bitwise_and(lax.shift_right_logical(fine_parents, LANE_BITS), shares - 1)
    table = hits(MOST_SHARES, 0, share_of).astype(jnp.bfloat16)
    spots = hits(LANES, 0, jnp.bitwise_and(fine_parents, LANES - 1)).astype(jnp.bfloat16)
    counts_ref[...] = lax.dot_general(
        table, spots, (((1,), (1,)), ((), ())), preferred_element_type=jnp.float32
    )
    place = jnp.bitwise_and(candidates_ref[...], fine_count - 1)
    chunk = lax.shift_right_logical(place, LANE_BITS)
    within = jnp.bitwise_and(place, LANES - 1)
    wide_ref[:, :feat_dim] = points_ref[...]
    wide_ref[:, feat_dim : feat_dim + LANES] = small(chunk)
    wide_ref[:, feat_dim + LANES : feat_dim + 2 * LANES] = small(within)
    every = lax.broadcasted_iota(jnp.int32, (1, devices), 1)
    sent = dot(hits(slots, 0, owners * slot_count + ranks).astype(jnp.bfloat16), points_ref[...])
    sent = sent + dot(hits(slots, 0, owners * slot_count + CAP).astype(jnp.bfloat16), id_rows)
    sent = sent + dot(hits(slots, 0, every * slot_count + CAP).astype(jnp.bfloat16), counts)
    out_ref[...] = sent.astype(jnp.bfloat16)


def outgoing(
    which, point_cluster, points, middle_parent, fine_parent, candidates, devices, fine_count
):
    rows, feat_dim = points.shape
    slots = devices * (CAP + 1)
    wide = feat_dim + 2 * LANES

    def whole(i, s):
        return (0, 0)

    return pl.pallas_call(
        functools.partial(send_kernel, fine_count=fine_count),
        out_shape=(
            jax.ShapeDtypeStruct((slots, feat_dim), jnp.bfloat16),
            jax.ShapeDtypeStruct((rows, wide), jnp.bfloat16),
            jax.ShapeDtypeStruct((MOST_SHARES, LANES), jnp.float32),
        ),
        grid_spec=pltpu.PrefetchScalarGridSpec(
            num_scalar_prefetch=1,
            grid=(1,),
            in_specs=[
                pl.BlockSpec((1, rows), whole),
                pl.BlockSpec((rows, feat_dim), whole),
                pl.BlockSpec((1, middle_parent.shape[0]), whole),
                pl.BlockSpec((1, fine_parent.shape[0]), whole),
                pl.BlockSpec(candidates.shape, whole),
            ],
            out_specs=[
                pl.BlockSpec((slots, feat_dim), whole),
                pl.BlockSpec((rows, wide), whole),
                pl.BlockSpec((MOST_SHARES, LANES), whole),
            ],
        ),
        compiler_params=pltpu.CompilerParams(vmem_limit_bytes=60 * 1024 * 1024),
        cost_estimate=pl.CostEstimate(
            flops=4 * slots * LANES * feat_dim, bytes_accessed=2 * 1024 * 1024, transcendentals=0
        ),
    )(
        which,
        point_cluster[None, :],
        points,
        middle_parent[None, :],
        fine_parent[None, :],
        candidates,
    )


def fine_step(step, got, ids_ref, old_fine, held):
    first = pl.multiple_of(step * FINE_STEP, FINE_STEP)
    found = hits(FINE_STEP, first, ids_ref[...])
    members = jnp.sum(found.astype(jnp.float32), axis=1, keepdims=True)
    totals = dot(found.astype(jnp.bfloat16), got) + old_fine.astype(jnp.float32)
    held[pl.ds(first, FINE_STEP), :] = (totals * (1.0 / (members + 1.0))).astype(jnp.bfloat16)


def left_kernel(got_ref, ids_ref, old_fine_ref, parent_ref, fine_ref, middle_ref, held, sent):
    step = pl.program_id(0)
    fine_steps = held.shape[0] // FINE_STEP
    store = pltpu.make_async_copy(held, fine_ref.at[:, : held.shape[1]], sent)

    @pl.when(step < fine_steps)
    def _():
        fine_step(step, got_ref[...], ids_ref, old_fine_ref[...], held)

    @pl.when(step == fine_steps)
    def _():
        store.start()

    @pl.when(step >= fine_steps)
    def _():
        first = (step - fine_steps) * LEFT_STEP
        table = quick_table(LEFT_STEP, first, parent_ref[...])
        middle_ref[...] = dot(table, held[...]).astype(jnp.bfloat16)

    @pl.when(step == pl.num_programs(0) - 1)
    def _():
        store.wait()


def left_levels(got, ids, old_fine, parents, middle_count):
    fine_count, feat_dim = old_fine.shape
    half = feat_dim // LEFT_PARTS
    slots = got.shape[0]
    fine_steps = fine_count // FINE_STEP

    def whole(i):
        return (0, 0)

    return pl.pallas_call(
        left_kernel,
        out_shape=(
            jax.ShapeDtypeStruct((fine_count, feat_dim), jnp.bfloat16),
            jax.ShapeDtypeStruct((middle_count, half), jnp.bfloat16),
        ),
        grid=(fine_steps + middle_count // LEFT_STEP,),
        in_specs=[
            pl.BlockSpec((slots, half), whole),
            pl.BlockSpec((1, slots), whole),
            pl.BlockSpec((FINE_STEP, half), lambda i: (jnp.minimum(i, fine_steps - 1), 0)),
            pl.BlockSpec((1, fine_count), whole),
        ],
        out_specs=[
            pl.BlockSpec(memory_space=pl.ANY),
            pl.BlockSpec((LEFT_STEP, half), lambda i: (jnp.maximum(i - fine_steps, 0), 0)),
        ],
        scratch_shapes=[
            pltpu.VMEM((fine_count, half), jnp.bfloat16),
            pltpu.SemaphoreType.DMA,
        ],
        compiler_params=pltpu.CompilerParams(vmem_limit_bytes=56 * 1024 * 1024),
        cost_estimate=pl.CostEstimate(
            flops=2 * half * fine_count * (slots + middle_count),
            bytes_accessed=8 * 1024 * 1024,
            transcendentals=0,
        ),
    )(got, ids, old_fine, parents)


def right_kernel(
    share_ref,
    got_ref,
    ids_ref,
    old_fine_ref,
    parent_ref,
    members_ref,
    old_share_ref,
    top_parent_ref,
    left_ref,
    kept_ref,
    fine_ref,
    middle_ref,
    top_ref,
    held,
    scaled,
    sent,
):
    del kept_ref
    step = pl.program_id(0)
    fine_steps = held.shape[0] // FINE_STEP
    middle_steps = scaled.shape[0] // MIDDLE_STEP
    top_rows = top_ref.shape[0]
    half = left_ref.shape[1]
    store = pltpu.make_async_copy(held, fine_ref.at[:, half:], sent)

    @pl.when(step < fine_steps)
    def _():
        fine_step(step, got_ref[:, half:], ids_ref, old_fine_ref[:, half:], held)

    @pl.when(step == fine_steps)
    def _():
        store.start()

    @pl.when(jnp.logical_and(step >= fine_steps, step < fine_steps + middle_steps))
    def _():
        first = pl.multiple_of((step - fine_steps) * MIDDLE_STEP, MIDDLE_STEP)
        part = dot(quick_table(MIDDLE_STEP, first, parent_ref[...]), held[...])
        middle_ref[...] = part.astype(jnp.bfloat16)
        block = (step - fine_steps) * (MIDDLE_STEP // LANES)
        rows = [members_ref[pl.ds(block + i, 1), :] for i in range(MIDDLE_STEP // LANES)]
        weights = 1.0 / (jnp.concatenate([column(row) for row in rows], axis=0) + 1.0)
        left = left_ref[...].astype(jnp.float32) * weights
        scaled[pl.ds(first, MIDDLE_STEP), :half] = left.astype(jnp.bfloat16)
        scaled[pl.ds(first, MIDDLE_STEP), half:] = (part * weights).astype(jnp.bfloat16)

    @pl.when(step >= fine_steps + middle_steps)
    def _():
        first = (step - fine_steps - middle_steps) * top_rows
        olds = old_share_ref[...].astype(jnp.float32)
        members = column(members_ref[pl.ds(share_ref[0], 1), :])
        olds = (olds * (1.0 / (members + 1.0))).astype(jnp.bfloat16)
        own = pl.ds(pl.multiple_of(share_ref[0] * LANES, LANES), LANES)
        own_table = quick_table(top_rows, first, top_parent_ref[:, own])
        table = quick_table(top_rows, first, top_parent_ref[...])
        top_ref[...] = dot(table, scaled[...]) + dot(own_table, olds)

    @pl.when(step == pl.num_programs(0) - 1)
    def _():
        store.wait()


def right_levels(
    which, got, ids, old_fine, parents, members, old_middle, top_parents, left, kept, top_count
):
    fine_count, feat_dim = old_fine.shape
    half = feat_dim // LEFT_PARTS
    rest = feat_dim - half
    middle_count = old_middle.shape[0]
    share_rows = members.shape[1]
    slots = got.shape[0]
    fine_steps = fine_count // FINE_STEP
    middle_steps = middle_count // MIDDLE_STEP
    top_steps = top_count // TOP_STEP

    def fine_at(i, s):
        return (jnp.minimum(i, fine_steps - 1), 0)

    def middle_at(i, s):
        return (jnp.clip(i - fine_steps, 0, middle_steps - 1), 0)

    def top_at(i, s):
        return (jnp.maximum(i - fine_steps - middle_steps, 0), 0)

    def whole(i, s):
        return (0, 0)

    flops = 2 * rest * (fine_count * slots + middle_count * (fine_count + 2 * top_count))
    return pl.pallas_call(
        right_kernel,
        out_shape=(
            jax.ShapeDtypeStruct((fine_count, feat_dim), jnp.bfloat16),
            jax.ShapeDtypeStruct((middle_count, rest), jnp.bfloat16),
            jax.ShapeDtypeStruct((top_count, feat_dim), jnp.float32),
        ),
        grid_spec=pltpu.PrefetchScalarGridSpec(
            num_scalar_prefetch=1,
            grid=(fine_steps + middle_steps + top_steps,),
            in_specs=[
                pl.BlockSpec((slots, feat_dim), whole),
                pl.BlockSpec((1, slots), whole),
                pl.BlockSpec((FINE_STEP, feat_dim), fine_at),
                pl.BlockSpec((1, fine_count), whole),
                pl.BlockSpec(members.shape, whole),
                pl.BlockSpec((share_rows, feat_dim), lambda i, s: (s[0], 0)),
                pl.BlockSpec((1, middle_count), whole),
                pl.BlockSpec((MIDDLE_STEP, half), middle_at),
                pl.BlockSpec(memory_space=pl.ANY),
            ],
            out_specs=[
                pl.BlockSpec(memory_space=pl.ANY),
                pl.BlockSpec((MIDDLE_STEP, rest), middle_at),
                pl.BlockSpec((TOP_STEP, feat_dim), top_at),
            ],
            scratch_shapes=[
                pltpu.VMEM((fine_count, rest), jnp.bfloat16),
                pltpu.VMEM((middle_count, feat_dim), jnp.bfloat16),
                pltpu.SemaphoreType.DMA,
            ],
        ),
        input_output_aliases={9: 0},
        compiler_params=pltpu.CompilerParams(vmem_limit_bytes=56 * 1024 * 1024),
        cost_estimate=pl.CostEstimate(
            flops=flops, bytes_accessed=14 * 1024 * 1024, transcendentals=0
        ),
    )(which, got, ids, old_fine, parents, members, old_middle, top_parents, left, kept)


def distance_kernel(share_ref, rows_ref, fine_ref, norms_ref, out_ref):
    fine_count, feat_dim = fine_ref.shape
    rows = rows_ref.shape[0]
    block = rows_ref[:, :feat_dim]
    wide = block.astype(jnp.float32)
    point_norms = jnp.sum(wide * wide, axis=1, keepdims=True)
    cross = lax.dot_general(
        block, fine_ref[...], (((1,), (1,)), ((), ())), preferred_element_type=jnp.float32
    )
    places = rows_ref[:, feat_dim : feat_dim + 2 * LANES].astype(jnp.float32).astype(jnp.int32)
    chunk = places[:, :LANES]
    lane = places[:, LANES:]
    picked = jnp.zeros((rows, LANES), jnp.float32)
    for c in range(fine_count // LANES):
        here = slice(c * LANES, (c + 1) * LANES)
        scores = norms_ref[:, here] - 2.0 * cross[:, here]
        found = jnp.take_along_axis(scores, lane, axis=1)
        picked = jnp.where(chunk == c, found, picked)
    column = lax.broadcasted_iota(jnp.int32, (rows, LANES), 1)
    mine = jnp.bitwise_and(column, share_ref[1] - 1) == share_ref[0]
    total = jnp.maximum(picked + point_norms, 0.0) * (1.0 / feat_dim)
    total = jnp.where(mine, total, 0.0)
    per_block = rows // out_ref.shape[0]
    for block in range(out_ref.shape[0]):
        packed = jnp.zeros((SUBLANES, LANES), jnp.float32)
        for b in range(per_block // SUBLANES):
            first = block * per_block + b * SUBLANES
            shift = jnp.bitwise_and(b - share_ref[0] + LANES, LANES - 1)
            packed = packed + pltpu.roll(total[first : first + SUBLANES], shift, 1)
        out_ref[block] = packed


def candidate_parts(share, all_rows, old_fine, fine_norms, groups):
    row_count = all_rows.shape[0] // groups
    fine_count, feat_dim = old_fine.shape
    per_step = 2
    return pl.pallas_call(
        distance_kernel,
        out_shape=jax.ShapeDtypeStruct((groups, SUBLANES, LANES), jnp.float32),
        grid_spec=pltpu.PrefetchScalarGridSpec(
            num_scalar_prefetch=1,
            grid=(groups // per_step,),
            in_specs=[
                pl.BlockSpec((per_step * row_count, all_rows.shape[1]), lambda i, s: (i, 0)),
                pl.BlockSpec((fine_count, feat_dim), lambda i, s: (0, 0)),
                pl.BlockSpec((1, fine_count), lambda i, s: (0, 0)),
            ],
            out_specs=pl.BlockSpec((per_step, SUBLANES, LANES), lambda i, s: (i, 0, 0)),
        ),
        compiler_params=pltpu.CompilerParams(vmem_limit_bytes=40 * 1024 * 1024),
        cost_estimate=pl.CostEstimate(
            flops=LONG,
            bytes_accessed=2 * (groups * row_count + fine_count) * feat_dim,
            transcendentals=0,
        ),
    )(share, all_rows, old_fine, fine_norms)


def place_kernel(at_ref, *refs):
    *pieces, out_ref = refs
    for i, piece in enumerate(pieces):
        row = pl.multiple_of(at_ref[i], piece.shape[0])
        out_ref[pl.ds(row, piece.shape[0]), :] = piece[...]


def all_blocks(block, total):
    places = lax.axis_size("grp")
    cores = places // SIDE
    onward = ring(places, cores, 1)
    backward = ring(places, cores, SIDE - 1)
    across = [(i, i ^ 1) for i in range(places)]
    rows = block.shape[0]
    half = rows // 2
    before = lax.ppermute(block, "grp", onward)
    after = lax.ppermute(block, "grp", backward)
    far_first = lax.ppermute(before[:half], "grp", onward)
    far_last = lax.ppermute(after[half:], "grp", backward)
    pieces = [block, before, after, far_first, far_last]
    pieces += [lax.ppermute(piece, "grp", across) for piece in pieces]
    me = lax.axis_index("grp")
    chip = me // cores
    starts = []
    for core in (me % cores, 1 - me % cores):
        for turn, shift in ((0, 0), (SIDE - 1, 0), (1, 0), (2, 0), (2, half)):
            starts.append(((chip + turn) % SIDE * cores + core) * rows + shift)
    return pl.pallas_call(
        place_kernel,
        out_shape=jax.ShapeDtypeStruct((total, block.shape[1]), block.dtype),
        grid_spec=pltpu.PrefetchScalarGridSpec(
            num_scalar_prefetch=1,
            grid=(1,),
            in_specs=[pl.BlockSpec(piece.shape, lambda i, at: (0, 0)) for piece in pieces],
            out_specs=pl.BlockSpec((total, block.shape[1]), lambda i, at: (0, 0)),
        ),
        compiler_params=pltpu.CompilerParams(vmem_limit_bytes=32 * 1024 * 1024),
        cost_estimate=pl.CostEstimate(flops=0, bytes_accessed=4 * 1024 * 1024, transcendentals=0),
    )(jnp.stack(starts).astype(jnp.int32), *pieces)


def per_device(
    points, point_cluster, candidates, old_fine, fine_parent, old_middle, middle_parent, old_top
):
    devices = lax.axis_size(BOTH)
    group_width = lax.axis_size("sub")
    share = lax.axis_index("sub")
    device = lax.axis_index(BOTH)
    row_count, feat_dim = points.shape
    fine_count = old_fine.shape[0]
    middle_count = old_middle.shape[0]
    top_count = old_top.shape[0]
    share_rows = middle_count // group_width
    top_rows = top_count // devices
    which = jnp.stack([share, jnp.int32(group_width), jnp.int32(top_rows.bit_length() - 1)])

    slot_count = CAP + 1
    send_rows, wide_rows, middle_members = outgoing(
        which,
        point_cluster,
        points,
        middle_parent,
        fine_parent,
        candidates,
        devices,
        fine_count,
    )
    got = swap(send_rows.reshape(devices, slot_count, feat_dim), BOTH)
    side = got[:, CAP, :LANES].astype(jnp.float32)
    got_high = side[:, :CAP].astype(jnp.int32)
    got_low = side[:, LOW_LANE : LOW_LANE + CAP].astype(jnp.int32)
    got_ids = jnp.where(got_high > 0, (got_high - 1) * (1 << ID_BITS) + got_low, -1)
    got_ids = jnp.pad(got_ids, ((0, 0), (0, 1)), constant_values=-1)
    top_totals = jnp.sum(side[:, COUNT_LANE : COUNT_LANE + top_rows], axis=0)

    all_rows = lax.all_gather(wide_rows, "sub", axis=0, tiled=True)
    for apart in (1, SIDE):
        around = [middle_members]
        for turn in range(1, SIDE):
            around.append(lax.ppermute(middle_members, "sub", ring(group_width, apart, turn)))
        middle_members = sum(around)

    middle_local = fine_parent - lax.axis_index("grp") * middle_count
    got = got.reshape(devices * slot_count, feat_dim)
    got_ids = got_ids.reshape(1, devices * slot_count)
    got_ids, middle_members = lax.optimization_barrier((got_ids, middle_members))
    parents = middle_local[None, :]
    half_fine, left = left_levels(got, got_ids, old_fine, parents, middle_count)
    new_fine, right, top_part = right_levels(
        which,
        got,
        got_ids,
        old_fine,
        parents,
        middle_members,
        old_middle,
        middle_parent[None, :],
        left,
        half_fine,
        top_count,
    )

    left = swap(left.reshape(group_width, share_rows, -1), "sub")
    right, left = lax.optimization_barrier((right, left))
    right = swap(right.reshape(group_width, share_rows, -1), "sub")
    wide_fine = old_fine.astype(jnp.float32)
    fine_norms = jnp.sum(wide_fine * wide_fine, axis=1)[None, :]
    found = candidate_parts(which, all_rows, old_fine, fine_norms, group_width)
    right, found = lax.optimization_barrier((right, found))
    share_totals = lax.dynamic_slice_in_dim(middle_members, share, 1).reshape(share_rows)
    old_share = lax.dynamic_slice_in_dim(old_middle, share * share_rows, share_rows)
    left_share, right_share = [
        level_update(jnp.sum(parts.astype(jnp.float32), axis=0), share_totals, olds)
        for parts, olds in zip((left, right), jnp.split(old_share, [feat_dim // LEFT_PARTS], axis=1))
    ]
    new_share = jnp.concatenate([left_share, right_share], axis=1)
    new_middle = copied(lax.all_gather(new_share, "sub", axis=0, tiled=True))

    top_block = lax.psum_scatter(top_part, "grp", scatter_dimension=0, tiled=True)
    top_pieces = top_block.reshape(group_width, top_rows, feat_dim)
    returned = swap(jnp.concatenate([top_pieces, found], axis=2), "sub")
    top_sums = jnp.sum(returned[:, :, :feat_dim], axis=0)
    packed = returned[:, :, feat_dim:].reshape(group_width, SUBLANES, -1, group_width)
    packed = packed[..., : row_count // SUBLANES]
    candidate_sq_distance = packed.transpose(3, 1, 2, 0).reshape(row_count, -1)
    old_rows = lax.dynamic_slice_in_dim(old_top, device * top_rows, top_rows)
    new_rows = level_update(top_sums, top_totals, old_rows)
    new_block = spread(new_rows, "sub").reshape(group_width * top_rows, feat_dim)
    new_top = all_blocks(new_block, top_count)
    return (new_fine, new_middle, new_top, candidate_sq_distance)


def solution(mesh):
    placed = (
        P(BOTH, None),
        P(BOTH),
        P(BOTH, None),
        P(BOTH, None),
        P(BOTH),
        P("grp", None),
        P("grp"),
        P(),
    )
    return jax.shard_map(
        per_device,
        mesh=mesh,
        in_specs=placed,
        out_specs=(P(BOTH, None), P("grp", None), P(), P(BOTH, None)),
        check_vma=False,
    )
```

```python
import functools

import jax
import jax.numpy as jnp
from jax import lax
from jax.experimental import pallas as pl
from jax.experimental.pallas import tpu as pltpu
from jax.sharding import PartitionSpec as P

CAP = 3
LANES = 128
SUBLANES = 8
LANE_BITS = 7
ID_BITS = 6
LOW_LANE = 8
COUNT_LANE = 16
FINE_STEP = 1024
MIDDLE_STEP = 512
TOP_STEP = 512
LEFT_STEP = 1024
EXACT = 256
SIDE = 4
MOST_SHARES = 16
COPY_CHUNKS = 8
LEFT_PARTS = 2
LONG = 1_000_000_000_000
BOTH = ("grp", "sub")


def level_update(totals, members, olds):
    return ((totals + olds.astype(jnp.float32)) / (members + 1.0)[:, None]).astype(jnp.bfloat16)


def swap(blocks, axes):
    return lax.all_to_all(blocks, axes, split_axis=0, concat_axis=0, tiled=True)


def spread(block, axes):
    copies = lax.axis_size(axes)
    return swap(jnp.broadcast_to(block[None], (copies,) + block.shape), axes)


def copy_kernel(in_ref, out_ref, held, got, sent):
    chunk = in_ref.shape[0] // COPY_CHUNKS
    loads, stores = [], []
    for i in range(COPY_CHUNKS):
        here = pl.ds(i * chunk, chunk)
        loads.append(pltpu.make_async_copy(in_ref.at[here], held.at[here], got.at[i]))
        stores.append(pltpu.make_async_copy(held.at[here], out_ref.at[here], sent.at[i]))
    for load in loads:
        load.start()
    for load, store in zip(loads, stores):
        load.wait()
        store.start()
    for store in stores:
        store.wait()


def copied(array):
    return pl.pallas_call(
        copy_kernel,
        out_shape=jax.ShapeDtypeStruct(array.shape, array.dtype),
        in_specs=[pl.BlockSpec(memory_space=pl.ANY)],
        out_specs=pl.BlockSpec(memory_space=pl.ANY),
        scratch_shapes=[
            pltpu.VMEM(array.shape, array.dtype),
            pltpu.SemaphoreType.DMA((COPY_CHUNKS,)),
            pltpu.SemaphoreType.DMA((COPY_CHUNKS,)),
        ],
        compiler_params=pltpu.CompilerParams(vmem_limit_bytes=60 * 1024 * 1024),
        cost_estimate=pl.CostEstimate(flops=0, bytes_accessed=4 * array.size, transcendentals=0),
    )(array)


def ring(count, apart, turn):
    pairs = []
    for i in range(count):
        place = i // apart % SIDE
        pairs.append((i, i + ((place + turn) % SIDE - place) * apart))
    return pairs


def dot(left, right):
    return jnp.dot(left, right, preferred_element_type=jnp.float32)


def hits(count, first, parents):
    rows = lax.broadcasted_iota(jnp.int32, (count, parents.shape[1]), 0) + first
    return rows == parents


def quick_table(rows, first, parents):
    pieces = []
    for begin in range(0, rows, EXACT):
        near = parents - (first + begin)
        near = jnp.where(jnp.logical_and(near >= 0, near < EXACT), near, -1)
        near = near.astype(jnp.float32).astype(jnp.bfloat16)
        ids = lax.broadcasted_iota(jnp.int32, (EXACT, parents.shape[1]), 0)
        ids = ids.astype(jnp.float32).astype(jnp.bfloat16)
        pieces.append(jnp.where(ids == near, jnp.bfloat16(1), jnp.bfloat16(0)))
    return jnp.concatenate(pieces, axis=0)


def column(row):
    count = row.shape[1]
    down = lax.broadcasted_iota(jnp.int32, (count, count), 0)
    along = lax.broadcasted_iota(jnp.int32, (count, count), 1)
    return jnp.sum(jnp.where(down == along, row, jnp.zeros_like(row)), axis=1, keepdims=True)


def small(numbers):
    return numbers.astype(jnp.float32).astype(jnp.bfloat16)


def send_kernel(
    share_ref,
    clusters_ref,
    points_ref,
    parents_ref,
    fine_parents_ref,
    candidates_ref,
    out_ref,
    wide_ref,
    counts_ref,
    *,
    fine_count,
):
    rows, feat_dim = points_ref.shape
    slots = out_ref.shape[0]
    slot_count = CAP + 1
    devices = slots // slot_count
    fine_bits = fine_count.bit_length() - 1
    clusters = clusters_ref[...]
    cluster_column = column(clusters)
    owners = lax.shift_right_logical(clusters, fine_bits)
    owner_column = lax.shift_right_logical(cluster_column, fine_bits)
    down = lax.broadcasted_iota(jnp.int32, (rows, rows), 0)
    along = lax.broadcasted_iota(jnp.int32, (rows, rows), 1)
    same = owner_column == owners
    ranks = jnp.sum(jnp.where(same & (down < along), 1, 0), axis=0, keepdims=True)
    rank_column = jnp.sum(jnp.where(same & (along < down), 1, 0), axis=1, keepdims=True)
    ids = jnp.bitwise_and(cluster_column, fine_count - 1)
    high = lax.shift_right_logical(ids, ID_BITS) + 1
    low = jnp.bitwise_and(ids, (1 << ID_BITS) - 1)
    lane = lax.broadcasted_iota(jnp.int32, (rows, feat_dim), 1)
    id_rows = jnp.where(lane == rank_column, high, jnp.where(lane == LOW_LANE + rank_column, low, 0))
    id_rows = id_rows.astype(jnp.float32).astype(jnp.bfloat16)
    share = share_ref[0]
    parents = parents_ref[:, pl.ds(pl.multiple_of(share * LANES, LANES), LANES)]
    top_bits = share_ref[2]
    table = hits(devices, 0, lax.shift_right_logical(parents, top_bits)).astype(jnp.bfloat16)
    within = jnp.bitwise_and(parents, lax.shift_left(jnp.int32(1), top_bits) - 1)
    spots = hits(feat_dim, 0, within + COUNT_LANE).astype(jnp.bfloat16)
    counts = lax.dot_general(
        table, spots, (((1,), (1,)), ((), ())), preferred_element_type=jnp.float32
    )
    counts = counts.astype(jnp.bfloat16)
    fine_parents = fine_parents_ref[...]
    shares = share_ref[1]
    share_of = jnp.bitwise_and(lax.shift_right_logical(fine_parents, LANE_BITS), shares - 1)
    table = hits(MOST_SHARES, 0, share_of).astype(jnp.bfloat16)
    spots = hits(LANES, 0, jnp.bitwise_and(fine_parents, LANES - 1)).astype(jnp.bfloat16)
    counts_ref[...] = lax.dot_general(
        table, spots, (((1,), (1,)), ((), ())), preferred_element_type=jnp.float32
    )
    place = jnp.bitwise_and(candidates_ref[...], fine_count - 1)
    chunk = lax.shift_right_logical(place, LANE_BITS)
    within = jnp.bitwise_and(place, LANES - 1)
    wide_ref[:, :feat_dim] = points_ref[...]
    wide_ref[:, feat_dim : feat_dim + LANES] = small(chunk)
    wide_ref[:, feat_dim + LANES : feat_dim + 2 * LANES] = small(within)
    every = lax.broadcasted_iota(jnp.int32, (1, devices), 1)
    sent = dot(hits(slots, 0, owners * slot_count + ranks).astype(jnp.bfloat16), points_ref[...])
    sent = sent + dot(hits(slots, 0, owners * slot_count + CAP).astype(jnp.bfloat16), id_rows)
    sent = sent + dot(hits(slots, 0, every * slot_count + CAP).astype(jnp.bfloat16), counts)
    out_ref[...] = sent.astype(jnp.bfloat16)


def outgoing(
    which, point_cluster, points, middle_parent, fine_parent, candidates, devices, fine_count
):
    rows, feat_dim = points.shape
    slots = devices * (CAP + 1)
    wide = feat_dim + 2 * LANES

    def whole(i, s):
        return (0, 0)

    return pl.pallas_call(
        functools.partial(send_kernel, fine_count=fine_count),
        out_shape=(
            jax.ShapeDtypeStruct((slots, feat_dim), jnp.bfloat16),
            jax.ShapeDtypeStruct((rows, wide), jnp.bfloat16),
            jax.ShapeDtypeStruct((MOST_SHARES, LANES), jnp.float32),
        ),
        grid_spec=pltpu.PrefetchScalarGridSpec(
            num_scalar_prefetch=1,
            grid=(1,),
            in_specs=[
                pl.BlockSpec((1, rows), whole),
                pl.BlockSpec((rows, feat_dim), whole),
                pl.BlockSpec((1, middle_parent.shape[0]), whole),
                pl.BlockSpec((1, fine_parent.shape[0]), whole),
                pl.BlockSpec(candidates.shape, whole),
            ],
            out_specs=[
                pl.BlockSpec((slots, feat_dim), whole),
                pl.BlockSpec((rows, wide), whole),
                pl.BlockSpec((MOST_SHARES, LANES), whole),
            ],
        ),
        compiler_params=pltpu.CompilerParams(vmem_limit_bytes=60 * 1024 * 1024),
        cost_estimate=pl.CostEstimate(
            flops=4 * slots * LANES * feat_dim, bytes_accessed=2 * 1024 * 1024, transcendentals=0
        ),
    )(
        which,
        point_cluster[None, :],
        points,
        middle_parent[None, :],
        fine_parent[None, :],
        candidates,
    )


def fine_step(step, got, ids_ref, old_fine, held):
    first = pl.multiple_of(step * FINE_STEP, FINE_STEP)
    found = hits(FINE_STEP, first, ids_ref[...])
    members = jnp.sum(found.astype(jnp.float32), axis=1, keepdims=True)
    totals = dot(found.astype(jnp.bfloat16), got) + old_fine.astype(jnp.float32)
    held[pl.ds(first, FINE_STEP), :] = (totals * (1.0 / (members + 1.0))).astype(jnp.bfloat16)


def left_kernel(got_ref, ids_ref, old_fine_ref, parent_ref, fine_ref, middle_ref, held, sent):
    step = pl.program_id(0)
    fine_steps = held.shape[0] // FINE_STEP
    store = pltpu.make_async_copy(held, fine_ref.at[:, : held.shape[1]], sent)

    @pl.when(step < fine_steps)
    def _():
        fine_step(step, got_ref[...], ids_ref, old_fine_ref[...], held)

    @pl.when(step == fine_steps)
    def _():
        store.start()

    @pl.when(step >= fine_steps)
    def _():
        first = (step - fine_steps) * LEFT_STEP
        table = quick_table(LEFT_STEP, first, parent_ref[...])
        middle_ref[...] = dot(table, held[...]).astype(jnp.bfloat16)

    @pl.when(step == pl.num_programs(0) - 1)
    def _():
        store.wait()


def left_levels(got, ids, old_fine, parents, middle_count):
    fine_count, feat_dim = old_fine.shape
    half = feat_dim // LEFT_PARTS
    slots = got.shape[0]
    fine_steps = fine_count // FINE_STEP

    def whole(i):
        return (0, 0)

    return pl.pallas_call(
        left_kernel,
        out_shape=(
            jax.ShapeDtypeStruct((fine_count, feat_dim), jnp.bfloat16),
            jax.ShapeDtypeStruct((middle_count, half), jnp.bfloat16),
        ),
        grid=(fine_steps + middle_count // LEFT_STEP,),
        in_specs=[
            pl.BlockSpec((slots, half), whole),
            pl.BlockSpec((1, slots), whole),
            pl.BlockSpec((FINE_STEP, half), lambda i: (jnp.minimum(i, fine_steps - 1), 0)),
            pl.BlockSpec((1, fine_count), whole),
        ],
        out_specs=[
            pl.BlockSpec(memory_space=pl.ANY),
            pl.BlockSpec((LEFT_STEP, half), lambda i: (jnp.maximum(i - fine_steps, 0), 0)),
        ],
        scratch_shapes=[
            pltpu.VMEM((fine_count, half), jnp.bfloat16),
            pltpu.SemaphoreType.DMA,
        ],
        compiler_params=pltpu.CompilerParams(vmem_limit_bytes=56 * 1024 * 1024),
        cost_estimate=pl.CostEstimate(
            flops=2 * half * fine_count * (slots + middle_count),
            bytes_accessed=8 * 1024 * 1024,
            transcendentals=0,
        ),
    )(got, ids, old_fine, parents)


def right_kernel(
    share_ref,
    got_ref,
    ids_ref,
    old_fine_ref,
    parent_ref,
    members_ref,
    old_share_ref,
    top_parent_ref,
    left_ref,
    kept_ref,
    fine_ref,
    middle_ref,
    top_ref,
    held,
    scaled,
    sent,
):
    del kept_ref
    step = pl.program_id(0)
    fine_steps = held.shape[0] // FINE_STEP
    middle_steps = scaled.shape[0] // MIDDLE_STEP
    top_rows = top_ref.shape[0]
    half = left_ref.shape[1]
    store = pltpu.make_async_copy(held, fine_ref.at[:, half:], sent)

    @pl.when(step < fine_steps)
    def _():
        fine_step(step, got_ref[:, half:], ids_ref, old_fine_ref[:, half:], held)

    @pl.when(step == fine_steps)
    def _():
        store.start()

    @pl.when(jnp.logical_and(step >= fine_steps, step < fine_steps + middle_steps))
    def _():
        first = pl.multiple_of((step - fine_steps) * MIDDLE_STEP, MIDDLE_STEP)
        part = dot(quick_table(MIDDLE_STEP, first, parent_ref[...]), held[...])
        middle_ref[...] = part.astype(jnp.bfloat16)
        block = (step - fine_steps) * (MIDDLE_STEP // LANES)
        rows = [members_ref[pl.ds(block + i, 1), :] for i in range(MIDDLE_STEP // LANES)]
        weights = 1.0 / (jnp.concatenate([column(row) for row in rows], axis=0) + 1.0)
        left = left_ref[...].astype(jnp.float32) * weights
        scaled[pl.ds(first, MIDDLE_STEP), :half] = left.astype(jnp.bfloat16)
        scaled[pl.ds(first, MIDDLE_STEP), half:] = (part * weights).astype(jnp.bfloat16)

    @pl.when(step >= fine_steps + middle_steps)
    def _():
        first = (step - fine_steps - middle_steps) * top_rows
        olds = old_share_ref[...].astype(jnp.float32)
        members = column(members_ref[pl.ds(share_ref[0], 1), :])
        olds = (olds * (1.0 / (members + 1.0))).astype(jnp.bfloat16)
        own = pl.ds(pl.multiple_of(share_ref[0] * LANES, LANES), LANES)
        own_table = quick_table(top_rows, first, top_parent_ref[:, own])
        table = quick_table(top_rows, first, top_parent_ref[...])
        top_ref[...] = dot(table, scaled[...]) + dot(own_table, olds)

    @pl.when(step == pl.num_programs(0) - 1)
    def _():
        store.wait()


def right_levels(
    which, got, ids, old_fine, parents, members, old_middle, top_parents, left, kept, top_count
):
    fine_count, feat_dim = old_fine.shape
    half = feat_dim // LEFT_PARTS
    rest = feat_dim - half
    middle_count = old_middle.shape[0]
    share_rows = members.shape[1]
    slots = got.shape[0]
    fine_steps = fine_count // FINE_STEP
    middle_steps = middle_count // MIDDLE_STEP
    top_steps = top_count // TOP_STEP

    def fine_at(i, s):
        return (jnp.minimum(i, fine_steps - 1), 0)

    def middle_at(i, s):
        return (jnp.clip(i - fine_steps, 0, middle_steps - 1), 0)

    def top_at(i, s):
        return (jnp.maximum(i - fine_steps - middle_steps, 0), 0)

    def whole(i, s):
        return (0, 0)

    flops = 2 * rest * (fine_count * slots + middle_count * (fine_count + 2 * top_count))
    return pl.pallas_call(
        right_kernel,
        out_shape=(
            jax.ShapeDtypeStruct((fine_count, feat_dim), jnp.bfloat16),
            jax.ShapeDtypeStruct((middle_count, rest), jnp.bfloat16),
            jax.ShapeDtypeStruct((top_count, feat_dim), jnp.float32),
        ),
        grid_spec=pltpu.PrefetchScalarGridSpec(
            num_scalar_prefetch=1,
            grid=(fine_steps + middle_steps + top_steps,),
            in_specs=[
                pl.BlockSpec((slots, feat_dim), whole),
                pl.BlockSpec((1, slots), whole),
                pl.BlockSpec((FINE_STEP, feat_dim), fine_at),
                pl.BlockSpec((1, fine_count), whole),
                pl.BlockSpec(members.shape, whole),
                pl.BlockSpec((share_rows, feat_dim), lambda i, s: (s[0], 0)),
                pl.BlockSpec((1, middle_count), whole),
                pl.BlockSpec((MIDDLE_STEP, half), middle_at),
                pl.BlockSpec(memory_space=pl.ANY),
            ],
            out_specs=[
                pl.BlockSpec(memory_space=pl.ANY),
                pl.BlockSpec((MIDDLE_STEP, rest), middle_at),
                pl.BlockSpec((TOP_STEP, feat_dim), top_at),
            ],
            scratch_shapes=[
                pltpu.VMEM((fine_count, rest), jnp.bfloat16),
                pltpu.VMEM((middle_count, feat_dim), jnp.bfloat16),
                pltpu.SemaphoreType.DMA,
            ],
        ),
        input_output_aliases={9: 0},
        compiler_params=pltpu.CompilerParams(vmem_limit_bytes=56 * 1024 * 1024),
        cost_estimate=pl.CostEstimate(
            flops=flops, bytes_accessed=14 * 1024 * 1024, transcendentals=0
        ),
    )(which, got, ids, old_fine, parents, members, old_middle, top_parents, left, kept)


def distance_kernel(share_ref, rows_ref, fine_ref, norms_ref, out_ref):
    fine_count, feat_dim = fine_ref.shape
    rows = rows_ref.shape[0]
    block = rows_ref[:, :feat_dim]
    wide = block.astype(jnp.float32)
    point_norms = jnp.sum(wide * wide, axis=1, keepdims=True)
    cross = lax.dot_general(
        block, fine_ref[...], (((1,), (1,)), ((), ())), preferred_element_type=jnp.float32
    )
    places = rows_ref[:, feat_dim : feat_dim + 2 * LANES].astype(jnp.float32).astype(jnp.int32)
    chunk = places[:, :LANES]
    lane = places[:, LANES:]
    picked = jnp.zeros((rows, LANES), jnp.float32)
    for c in range(fine_count // LANES):
        here = slice(c * LANES, (c + 1) * LANES)
        scores = norms_ref[:, here] - 2.0 * cross[:, here]
        found = jnp.take_along_axis(scores, lane, axis=1)
        picked = jnp.where(chunk == c, found, picked)
    column = lax.broadcasted_iota(jnp.int32, (rows, LANES), 1)
    mine = jnp.bitwise_and(column, share_ref[1] - 1) == share_ref[0]
    total = jnp.maximum(picked + point_norms, 0.0) * (1.0 / feat_dim)
    total = jnp.where(mine, total, 0.0)
    per_block = rows // out_ref.shape[0]
    for block in range(out_ref.shape[0]):
        packed = jnp.zeros((SUBLANES, LANES), jnp.float32)
        for b in range(per_block // SUBLANES):
            first = block * per_block + b * SUBLANES
            shift = jnp.bitwise_and(b - share_ref[0] + LANES, LANES - 1)
            packed = packed + pltpu.roll(total[first : first + SUBLANES], shift, 1)
        out_ref[block] = packed


def candidate_parts(share, all_rows, old_fine, fine_norms, groups):
    row_count = all_rows.shape[0] // groups
    fine_count, feat_dim = old_fine.shape
    per_step = 2
    return pl.pallas_call(
        distance_kernel,
        out_shape=jax.ShapeDtypeStruct((groups, SUBLANES, LANES), jnp.float32),
        grid_spec=pltpu.PrefetchScalarGridSpec(
            num_scalar_prefetch=1,
            grid=(groups // per_step,),
            in_specs=[
                pl.BlockSpec((per_step * row_count, all_rows.shape[1]), lambda i, s: (i, 0)),
                pl.BlockSpec((fine_count, feat_dim), lambda i, s: (0, 0)),
                pl.BlockSpec((1, fine_count), lambda i, s: (0, 0)),
            ],
            out_specs=pl.BlockSpec((per_step, SUBLANES, LANES), lambda i, s: (i, 0, 0)),
        ),
        compiler_params=pltpu.CompilerParams(vmem_limit_bytes=40 * 1024 * 1024),
        cost_estimate=pl.CostEstimate(
            flops=LONG,
            bytes_accessed=2 * (groups * row_count + fine_count) * feat_dim,
            transcendentals=0,
        ),
    )(share, all_rows, old_fine, fine_norms)


def place_kernel(at_ref, *refs):
    *pieces, out_ref = refs
    for i, piece in enumerate(pieces):
        row = pl.multiple_of(at_ref[i], piece.shape[0])
        out_ref[pl.ds(row, piece.shape[0]), :] = piece[...]


def all_blocks(block, total):
    places = lax.axis_size("grp")
    cores = places // SIDE
    onward = ring(places, cores, 1)
    backward = ring(places, cores, SIDE - 1)
    across = [(i, i ^ 1) for i in range(places)]
    rows = block.shape[0]
    half = rows // 2
    before = lax.ppermute(block, "grp", onward)
    after = lax.ppermute(block, "grp", backward)
    far_first = lax.ppermute(before[:half], "grp", onward)
    far_last = lax.ppermute(after[half:], "grp", backward)
    pieces = [block, before, after, far_first, far_last]
    pieces += [lax.ppermute(piece, "grp", across) for piece in pieces]
    me = lax.axis_index("grp")
    chip = me // cores
    starts = []
    for core in (me % cores, 1 - me % cores):
        for turn, shift in ((0, 0), (SIDE - 1, 0), (1, 0), (2, 0), (2, half)):
            starts.append(((chip + turn) % SIDE * cores + core) * rows + shift)
    return pl.pallas_call(
        place_kernel,
        out_shape=jax.ShapeDtypeStruct((total, block.shape[1]), block.dtype),
        grid_spec=pltpu.PrefetchScalarGridSpec(
            num_scalar_prefetch=1,
            grid=(1,),
            in_specs=[pl.BlockSpec(piece.shape, lambda i, at: (0, 0)) for piece in pieces],
            out_specs=pl.BlockSpec((total, block.shape[1]), lambda i, at: (0, 0)),
        ),
        compiler_params=pltpu.CompilerParams(vmem_limit_bytes=32 * 1024 * 1024),
        cost_estimate=pl.CostEstimate(flops=0, bytes_accessed=4 * 1024 * 1024, transcendentals=0),
    )(jnp.stack(starts).astype(jnp.int32), *pieces)


def per_device(
    points, point_cluster, candidates, old_fine, fine_parent, old_middle, middle_parent, old_top
):
    devices = lax.axis_size(BOTH)
    group_width = lax.axis_size("sub")
    share = lax.axis_index("sub")
    device = lax.axis_index(BOTH)
    row_count, feat_dim = points.shape
    fine_count = old_fine.shape[0]
    middle_count = old_middle.shape[0]
    top_count = old_top.shape[0]
    share_rows = middle_count // group_width
    top_rows = top_count // devices
    which = jnp.stack([share, jnp.int32(group_width), jnp.int32(top_rows.bit_length() - 1)])

    slot_count = CAP + 1
    send_rows, wide_rows, middle_members = outgoing(
        which,
        point_cluster,
        points,
        middle_parent,
        fine_parent,
        candidates,
        devices,
        fine_count,
    )
    got = swap(send_rows.reshape(devices, slot_count, feat_dim), BOTH)
    side = got[:, CAP, :LANES].astype(jnp.float32)
    got_high = side[:, :CAP].astype(jnp.int32)
    got_low = side[:, LOW_LANE : LOW_LANE + CAP].astype(jnp.int32)
    got_ids = jnp.where(got_high > 0, (got_high - 1) * (1 << ID_BITS) + got_low, -1)
    got_ids = jnp.pad(got_ids, ((0, 0), (0, 1)), constant_values=-1)
    top_totals = jnp.sum(side[:, COUNT_LANE : COUNT_LANE + top_rows], axis=0)

    all_rows = lax.all_gather(wide_rows, "sub", axis=0, tiled=True)
    for apart in (1, SIDE):
        around = [middle_members]
        for turn in range(1, SIDE):
            around.append(lax.ppermute(middle_members, "sub", ring(group_width, apart, turn)))
        middle_members = sum(around)

    middle_local = fine_parent - lax.axis_index("grp") * middle_count
    got = got.reshape(devices * slot_count, feat_dim)
    got_ids = got_ids.reshape(1, devices * slot_count)
    got_ids, middle_members = lax.optimization_barrier((got_ids, middle_members))
    parents = middle_local[None, :]
    half_fine, left = left_levels(got, got_ids, old_fine, parents, middle_count)
    new_fine, right, top_part = right_levels(
        which,
        got,
        got_ids,
        old_fine,
        parents,
        middle_members,
        old_middle,
        middle_parent[None, :],
        left,
        half_fine,
        top_count,
    )

    left = swap(left.reshape(group_width, share_rows, -1), "sub")
    right, left = lax.optimization_barrier((right, left))
    right = swap(right.reshape(group_width, share_rows, -1), "sub")
    wide_fine = old_fine.astype(jnp.float32)
    fine_norms = jnp.sum(wide_fine * wide_fine, axis=1)[None, :]
    found = candidate_parts(which, all_rows, old_fine, fine_norms, group_width)
    right, found = lax.optimization_barrier((right, found))
    share_totals = lax.dynamic_slice_in_dim(middle_members, share, 1).reshape(share_rows)
    old_share = lax.dynamic_slice_in_dim(old_middle, share * share_rows, share_rows)
    left_share, right_share = [
        level_update(jnp.sum(parts.astype(jnp.float32), axis=0), share_totals, olds)
        for parts, olds in zip((left, right), jnp.split(old_share, [feat_dim // LEFT_PARTS], axis=1))
    ]
    new_share = jnp.concatenate([left_share, right_share], axis=1)
    new_middle = copied(lax.all_gather(new_share, "sub", axis=0, tiled=True))

    top_block = lax.psum_scatter(top_part, "grp", scatter_dimension=0, tiled=True)
    top_pieces = top_block.reshape(group_width, top_rows, feat_dim)
    returned = swap(jnp.concatenate([top_pieces, found], axis=2), "sub")
    top_sums = jnp.sum(returned[:, :, :feat_dim], axis=0)
    packed = returned[:, :, feat_dim:].reshape(group_width, SUBLANES, -1, group_width)
    packed = packed[..., : row_count // SUBLANES]
    candidate_sq_distance = packed.transpose(3, 1, 2, 0).reshape(row_count, -1)
    old_rows = lax.dynamic_slice_in_dim(old_top, device * top_rows, top_rows)
    new_rows = level_update(top_sums, top_totals, old_rows)
    new_block = spread(new_rows, "sub").reshape(group_width * top_rows, feat_dim)
    new_top = all_blocks(new_block, top_count)
    return (new_fine, new_middle, new_top, candidate_sq_distance)


def solution(mesh):
    placed = (
        P(BOTH, None),
        P(BOTH),
        P(BOTH, None),
        P(BOTH, None),
        P(BOTH),
        P("grp", None),
        P("grp"),
        P(),
    )
    return jax.shard_map(
        per_device,
        mesh=mesh,
        in_specs=placed,
        out_specs=(P(BOTH, None), P("grp", None), P(), P(BOTH, None)),
        check_vma=False,
    )
```

```python
import functools

import jax
import jax.numpy as jnp
from jax import lax
from jax.experimental import pallas as pl
from jax.experimental.pallas import tpu as pltpu
from jax.sharding import PartitionSpec as P

CAP = 3
LANES = 128
SUBLANES = 8
LANE_BITS = 7
ID_BITS = 6
LOW_LANE = 8
COUNT_LANE = 16
FINE_STEP = 1024
MIDDLE_STEP = 512
TOP_STEP = 512
LEFT_STEP = 1024
EXACT = 256
SIDE = 4
MOST_SHARES = 16
COPY_CHUNKS = 16
LEFT_EIGHTHS = 3
LONG = 1_000_000_000_000
BOTH = ("grp", "sub")


def level_update(totals, members, olds):
    return ((totals + olds.astype(jnp.float32)) / (members + 1.0)[:, None]).astype(jnp.bfloat16)


def swap(blocks, axes):
    return lax.all_to_all(blocks, axes, split_axis=0, concat_axis=0, tiled=True)


def spread(block, axes):
    copies = lax.axis_size(axes)
    return swap(jnp.broadcast_to(block[None], (copies,) + block.shape), axes)


def copy_kernel(in_ref, out_ref, held, got, sent):
    chunk = in_ref.shape[0] // COPY_CHUNKS
    loads, stores = [], []
    for i in range(COPY_CHUNKS):
        here = pl.ds(i * chunk, chunk)
        loads.append(pltpu.make_async_copy(in_ref.at[here], held.at[here], got.at[i]))
        stores.append(pltpu.make_async_copy(held.at[here], out_ref.at[here], sent.at[i]))
    for load in loads:
        load.start()
    for load, store in zip(loads, stores):
        load.wait()
        store.start()
    for store in stores:
        store.wait()


def copied(array):
    return pl.pallas_call(
        copy_kernel,
        out_shape=jax.ShapeDtypeStruct(array.shape, array.dtype),
        in_specs=[pl.BlockSpec(memory_space=pl.ANY)],
        out_specs=pl.BlockSpec(memory_space=pl.ANY),
        scratch_shapes=[
            pltpu.VMEM(array.shape, array.dtype),
            pltpu.SemaphoreType.DMA((COPY_CHUNKS,)),
            pltpu.SemaphoreType.DMA((COPY_CHUNKS,)),
        ],
        compiler_params=pltpu.CompilerParams(vmem_limit_bytes=60 * 1024 * 1024),
        cost_estimate=pl.CostEstimate(flops=0, bytes_accessed=4 * array.size, transcendentals=0),
    )(array)


def ring(count, apart, turn):
    pairs = []
    for i in range(count):
        place = i // apart % SIDE
        pairs.append((i, i + ((place + turn) % SIDE - place) * apart))
    return pairs


def dot(left, right):
    return jnp.dot(left, right, preferred_element_type=jnp.float32)


def hits(count, first, parents):
    rows = lax.broadcasted_iota(jnp.int32, (count, parents.shape[1]), 0) + first
    return rows == parents


def quick_table(rows, first, parents):
    pieces = []
    for begin in range(0, rows, EXACT):
        near = parents - (first + begin)
        near = jnp.where(jnp.logical_and(near >= 0, near < EXACT), near, -1)
        near = near.astype(jnp.float32).astype(jnp.bfloat16)
        ids = lax.broadcasted_iota(jnp.int32, (EXACT, parents.shape[1]), 0)
        ids = ids.astype(jnp.float32).astype(jnp.bfloat16)
        pieces.append(jnp.where(ids == near, jnp.bfloat16(1), jnp.bfloat16(0)))
    return jnp.concatenate(pieces, axis=0)


def column(row):
    count = row.shape[1]
    down = lax.broadcasted_iota(jnp.int32, (count, count), 0)
    along = lax.broadcasted_iota(jnp.int32, (count, count), 1)
    return jnp.sum(jnp.where(down == along, row, jnp.zeros_like(row)), axis=1, keepdims=True)


def small(numbers):
    return numbers.astype(jnp.float32).astype(jnp.bfloat16)


def send_kernel(
    share_ref,
    clusters_ref,
    points_ref,
    parents_ref,
    fine_parents_ref,
    candidates_ref,
    out_ref,
    wide_ref,
    counts_ref,
    *,
    fine_count,
):
    rows, feat_dim = points_ref.shape
    slots = out_ref.shape[0]
    slot_count = CAP + 1
    devices = slots // slot_count
    fine_bits = fine_count.bit_length() - 1
    clusters = clusters_ref[...]
    cluster_column = column(clusters)
    owners = lax.shift_right_logical(clusters, fine_bits)
    owner_column = lax.shift_right_logical(cluster_column, fine_bits)
    down = lax.broadcasted_iota(jnp.int32, (rows, rows), 0)
    along = lax.broadcasted_iota(jnp.int32, (rows, rows), 1)
    same = owner_column == owners
    ranks = jnp.sum(jnp.where(same & (down < along), 1, 0), axis=0, keepdims=True)
    rank_column = jnp.sum(jnp.where(same & (along < down), 1, 0), axis=1, keepdims=True)
    ids = jnp.bitwise_and(cluster_column, fine_count - 1)
    high = lax.shift_right_logical(ids, ID_BITS) + 1
    low = jnp.bitwise_and(ids, (1 << ID_BITS) - 1)
    lane = lax.broadcasted_iota(jnp.int32, (rows, feat_dim), 1)
    id_rows = jnp.where(lane == rank_column, high, jnp.where(lane == LOW_LANE + rank_column, low, 0))
    id_rows = id_rows.astype(jnp.float32).astype(jnp.bfloat16)
    share = share_ref[0]
    parents = parents_ref[:, pl.ds(pl.multiple_of(share * LANES, LANES), LANES)]
    top_bits = share_ref[2]
    table = hits(devices, 0, lax.shift_right_logical(parents, top_bits)).astype(jnp.bfloat16)
    within = jnp.bitwise_and(parents, lax.shift_left(jnp.int32(1), top_bits) - 1)
    spots = hits(feat_dim, 0, within + COUNT_LANE).astype(jnp.bfloat16)
    counts = lax.dot_general(
        table, spots, (((1,), (1,)), ((), ())), preferred_element_type=jnp.float32
    )
    counts = counts.astype(jnp.bfloat16)
    fine_parents = fine_parents_ref[...]
    shares = share_ref[1]
    share_of = jnp.bitwise_and(lax.shift_right_logical(fine_parents, LANE_BITS), shares - 1)
    table = hits(MOST_SHARES, 0, share_of).astype(jnp.bfloat16)
    spots = hits(LANES, 0, jnp.bitwise_and(fine_parents, LANES - 1)).astype(jnp.bfloat16)
    counts_ref[...] = lax.dot_general(
        table, spots, (((1,), (1,)), ((), ())), preferred_element_type=jnp.float32
    )
    place = jnp.bitwise_and(candidates_ref[...], fine_count - 1)
    chunk = lax.shift_right_logical(place, LANE_BITS)
    within = jnp.bitwise_and(place, LANES - 1)
    wide_ref[:, :feat_dim] = points_ref[...]
    wide_ref[:, feat_dim : feat_dim + LANES] = small(chunk)
    wide_ref[:, feat_dim + LANES : feat_dim + 2 * LANES] = small(within)
    every = lax.broadcasted_iota(jnp.int32, (1, devices), 1)
    sent = dot(hits(slots, 0, owners * slot_count + ranks).astype(jnp.bfloat16), points_ref[...])
    sent = sent + dot(hits(slots, 0, owners * slot_count + CAP).astype(jnp.bfloat16), id_rows)
    sent = sent + dot(hits(slots, 0, every * slot_count + CAP).astype(jnp.bfloat16), counts)
    out_ref[...] = sent.astype(jnp.bfloat16)


def outgoing(
    which, point_cluster, points, middle_parent, fine_parent, candidates, devices, fine_count
):
    rows, feat_dim = points.shape
    slots = devices * (CAP + 1)
    wide = feat_dim + 2 * LANES

    def whole(i, s):
        return (0, 0)

    return pl.pallas_call(
        functools.partial(send_kernel, fine_count=fine_count),
        out_shape=(
            jax.ShapeDtypeStruct((slots, feat_dim), jnp.bfloat16),
            jax.ShapeDtypeStruct((rows, wide), jnp.bfloat16),
            jax.ShapeDtypeStruct((MOST_SHARES, LANES), jnp.float32),
        ),
        grid_spec=pltpu.PrefetchScalarGridSpec(
            num_scalar_prefetch=1,
            grid=(1,),
            in_specs=[
                pl.BlockSpec((1, rows), whole),
                pl.BlockSpec((rows, feat_dim), whole),
                pl.BlockSpec((1, middle_parent.shape[0]), whole),
                pl.BlockSpec((1, fine_parent.shape[0]), whole),
                pl.BlockSpec(candidates.shape, whole),
            ],
            out_specs=[
                pl.BlockSpec((slots, feat_dim), whole),
                pl.BlockSpec((rows, wide), whole),
                pl.BlockSpec((MOST_SHARES, LANES), whole),
            ],
        ),
        compiler_params=pltpu.CompilerParams(vmem_limit_bytes=60 * 1024 * 1024),
        cost_estimate=pl.CostEstimate(
            flops=4 * slots * LANES * feat_dim, bytes_accessed=2 * 1024 * 1024, transcendentals=0
        ),
    )(
        which,
        point_cluster[None, :],
        points,
        middle_parent[None, :],
        fine_parent[None, :],
        candidates,
    )


def fine_step(step, got, ids_ref, old_fine, held):
    first = pl.multiple_of(step * FINE_STEP, FINE_STEP)
    found = hits(FINE_STEP, first, ids_ref[...])
    members = jnp.sum(found.astype(jnp.float32), axis=1, keepdims=True)
    totals = dot(found.astype(jnp.bfloat16), got) + old_fine.astype(jnp.float32)
    held[pl.ds(first, FINE_STEP), :] = (totals * (1.0 / (members + 1.0))).astype(jnp.bfloat16)


def left_kernel(got_ref, ids_ref, old_fine_ref, parent_ref, fine_ref, middle_ref, held, sent):
    step = pl.program_id(0)
    fine_steps = held.shape[0] // FINE_STEP
    store = pltpu.make_async_copy(held, fine_ref.at[:, : held.shape[1]], sent)

    @pl.when(step < fine_steps)
    def _():
        fine_step(step, got_ref[...], ids_ref, old_fine_ref[...], held)

    @pl.when(step == fine_steps)
    def _():
        store.start()

    @pl.when(step >= fine_steps)
    def _():
        first = (step - fine_steps) * LEFT_STEP
        table = quick_table(LEFT_STEP, first, parent_ref[...])
        middle_ref[...] = dot(table, held[...]).astype(jnp.bfloat16)

    @pl.when(step == pl.num_programs(0) - 1)
    def _():
        store.wait()


def left_levels(got, ids, old_fine, parents, middle_count):
    fine_count, feat_dim = old_fine.shape
    half = feat_dim // 8 * LEFT_EIGHTHS
    slots = got.shape[0]
    fine_steps = fine_count // FINE_STEP

    def whole(i):
        return (0, 0)

    return pl.pallas_call(
        left_kernel,
        out_shape=(
            jax.ShapeDtypeStruct((fine_count, feat_dim), jnp.bfloat16),
            jax.ShapeDtypeStruct((middle_count, half), jnp.bfloat16),
        ),
        grid=(fine_steps + middle_count // LEFT_STEP,),
        in_specs=[
            pl.BlockSpec((slots, half), whole),
            pl.BlockSpec((1, slots), whole),
            pl.BlockSpec((FINE_STEP, half), lambda i: (jnp.minimum(i, fine_steps - 1), 0)),
            pl.BlockSpec((1, fine_count), whole),
        ],
        out_specs=[
            pl.BlockSpec(memory_space=pl.ANY),
            pl.BlockSpec((LEFT_STEP, half), lambda i: (jnp.maximum(i - fine_steps, 0), 0)),
        ],
        scratch_shapes=[
            pltpu.VMEM((fine_count, half), jnp.bfloat16),
            pltpu.SemaphoreType.DMA,
        ],
        compiler_params=pltpu.CompilerParams(vmem_limit_bytes=56 * 1024 * 1024),
        cost_estimate=pl.CostEstimate(
            flops=2 * half * fine_count * (slots + middle_count),
            bytes_accessed=8 * 1024 * 1024,
            transcendentals=0,
        ),
    )(got, ids, old_fine, parents)


def right_kernel(
    share_ref,
    got_ref,
    ids_ref,
    old_fine_ref,
    parent_ref,
    members_ref,
    old_share_ref,
    top_parent_ref,
    left_ref,
    kept_ref,
    fine_ref,
    middle_ref,
    top_ref,
    held,
    scaled,
    sent,
):
    del kept_ref
    step = pl.program_id(0)
    fine_steps = held.shape[0] // FINE_STEP
    middle_steps = scaled.shape[0] // MIDDLE_STEP
    top_rows = top_ref.shape[0]
    half = left_ref.shape[1]
    store = pltpu.make_async_copy(held, fine_ref.at[:, half:], sent)

    @pl.when(step < fine_steps)
    def _():
        fine_step(step, got_ref[:, half:], ids_ref, old_fine_ref[:, half:], held)

    @pl.when(step == fine_steps)
    def _():
        store.start()

    @pl.when(jnp.logical_and(step >= fine_steps, step < fine_steps + middle_steps))
    def _():
        first = pl.multiple_of((step - fine_steps) * MIDDLE_STEP, MIDDLE_STEP)
        part = dot(quick_table(MIDDLE_STEP, first, parent_ref[...]), held[...])
        middle_ref[...] = part.astype(jnp.bfloat16)
        block = (step - fine_steps) * (MIDDLE_STEP // LANES)
        rows = [members_ref[pl.ds(block + i, 1), :] for i in range(MIDDLE_STEP // LANES)]
        weights = 1.0 / (jnp.concatenate([column(row) for row in rows], axis=0) + 1.0)
        left = left_ref[...].astype(jnp.float32) * weights
        scaled[pl.ds(first, MIDDLE_STEP), :half] = left.astype(jnp.bfloat16)
        scaled[pl.ds(first, MIDDLE_STEP), half:] = (part * weights).astype(jnp.bfloat16)

    @pl.when(step >= fine_steps + middle_steps)
    def _():
        first = (step - fine_steps - middle_steps) * top_rows
        olds = old_share_ref[...].astype(jnp.float32)
        members = column(members_ref[pl.ds(share_ref[0], 1), :])
        olds = (olds * (1.0 / (members + 1.0))).astype(jnp.bfloat16)
        own = pl.ds(pl.multiple_of(share_ref[0] * LANES, LANES), LANES)
        own_table = quick_table(top_rows, first, top_parent_ref[:, own])
        table = quick_table(top_rows, first, top_parent_ref[...])
        top_ref[...] = dot(table, scaled[...]) + dot(own_table, olds)

    @pl.when(step == pl.num_programs(0) - 1)
    def _():
        store.wait()


def right_levels(
    which, got, ids, old_fine, parents, members, old_middle, top_parents, left, kept, top_count
):
    fine_count, feat_dim = old_fine.shape
    half = feat_dim // 8 * LEFT_EIGHTHS
    rest = feat_dim - half
    middle_count = old_middle.shape[0]
    share_rows = members.shape[1]
    slots = got.shape[0]
    fine_steps = fine_count // FINE_STEP
    middle_steps = middle_count // MIDDLE_STEP
    top_steps = top_count // TOP_STEP

    def fine_at(i, s):
        return (jnp.minimum(i, fine_steps - 1), 0)

    def middle_at(i, s):
        return (jnp.clip(i - fine_steps, 0, middle_steps - 1), 0)

    def top_at(i, s):
        return (jnp.maximum(i - fine_steps - middle_steps, 0), 0)

    def whole(i, s):
        return (0, 0)

    flops = 2 * rest * (fine_count * slots + middle_count * (fine_count + 2 * top_count))
    return pl.pallas_call(
        right_kernel,
        out_shape=(
            jax.ShapeDtypeStruct((fine_count, feat_dim), jnp.bfloat16),
            jax.ShapeDtypeStruct((middle_count, rest), jnp.bfloat16),
            jax.ShapeDtypeStruct((top_count, feat_dim), jnp.float32),
        ),
        grid_spec=pltpu.PrefetchScalarGridSpec(
            num_scalar_prefetch=1,
            grid=(fine_steps + middle_steps + top_steps,),
            in_specs=[
                pl.BlockSpec((slots, feat_dim), whole),
                pl.BlockSpec((1, slots), whole),
                pl.BlockSpec((FINE_STEP, feat_dim), fine_at),
                pl.BlockSpec((1, fine_count), whole),
                pl.BlockSpec(members.shape, whole),
                pl.BlockSpec((share_rows, feat_dim), lambda i, s: (s[0], 0)),
                pl.BlockSpec((1, middle_count), whole),
                pl.BlockSpec((MIDDLE_STEP, half), middle_at),
                pl.BlockSpec(memory_space=pl.ANY),
            ],
            out_specs=[
                pl.BlockSpec(memory_space=pl.ANY),
                pl.BlockSpec((MIDDLE_STEP, rest), middle_at),
                pl.BlockSpec((TOP_STEP, feat_dim), top_at),
            ],
            scratch_shapes=[
                pltpu.VMEM((fine_count, rest), jnp.bfloat16),
                pltpu.VMEM((middle_count, feat_dim), jnp.bfloat16),
                pltpu.SemaphoreType.DMA,
            ],
        ),
        input_output_aliases={9: 0},
        compiler_params=pltpu.CompilerParams(vmem_limit_bytes=56 * 1024 * 1024),
        cost_estimate=pl.CostEstimate(
            flops=flops, bytes_accessed=14 * 1024 * 1024, transcendentals=0
        ),
    )(which, got, ids, old_fine, parents, members, old_middle, top_parents, left, kept)


def distance_kernel(share_ref, rows_ref, fine_ref, norms_ref, out_ref):
    fine_count, feat_dim = fine_ref.shape
    rows = rows_ref.shape[0]
    block = rows_ref[:, :feat_dim]
    wide = block.astype(jnp.float32)
    point_norms = jnp.sum(wide * wide, axis=1, keepdims=True)
    cross = lax.dot_general(
        block, fine_ref[...], (((1,), (1,)), ((), ())), preferred_element_type=jnp.float32
    )
    places = rows_ref[:, feat_dim : feat_dim + 2 * LANES].astype(jnp.float32).astype(jnp.int32)
    chunk = places[:, :LANES]
    lane = places[:, LANES:]
    picked = jnp.zeros((rows, LANES), jnp.float32)
    for c in range(fine_count // LANES):
        here = slice(c * LANES, (c + 1) * LANES)
        scores = norms_ref[:, here] - 2.0 * cross[:, here]
        found = jnp.take_along_axis(scores, lane, axis=1)
        picked = jnp.where(chunk == c, found, picked)
    column = lax.broadcasted_iota(jnp.int32, (rows, LANES), 1)
    mine = jnp.bitwise_and(column, share_ref[1] - 1) == share_ref[0]
    total = jnp.maximum(picked + point_norms, 0.0) * (1.0 / feat_dim)
    total = jnp.where(mine, total, 0.0)
    per_block = rows // out_ref.shape[0]
    for block in range(out_ref.shape[0]):
        packed = jnp.zeros((SUBLANES, LANES), jnp.float32)
        for b in range(per_block // SUBLANES):
            first = block * per_block + b * SUBLANES
            shift = jnp.bitwise_and(b - share_ref[0] + LANES, LANES - 1)
            packed = packed + pltpu.roll(total[first : first + SUBLANES], shift, 1)
        out_ref[block] = packed


def candidate_parts(share, all_rows, old_fine, fine_norms, groups):
    row_count = all_rows.shape[0] // groups
    fine_count, feat_dim = old_fine.shape
    per_step = 2
    return pl.pallas_call(
        distance_kernel,
        out_shape=jax.ShapeDtypeStruct((groups, SUBLANES, LANES), jnp.float32),
        grid_spec=pltpu.PrefetchScalarGridSpec(
            num_scalar_prefetch=1,
            grid=(groups // per_step,),
            in_specs=[
                pl.BlockSpec((per_step * row_count, all_rows.shape[1]), lambda i, s: (i, 0)),
                pl.BlockSpec((fine_count, feat_dim), lambda i, s: (0, 0)),
                pl.BlockSpec((1, fine_count), lambda i, s: (0, 0)),
            ],
            out_specs=pl.BlockSpec((per_step, SUBLANES, LANES), lambda i, s: (i, 0, 0)),
        ),
        compiler_params=pltpu.CompilerParams(vmem_limit_bytes=40 * 1024 * 1024),
        cost_estimate=pl.CostEstimate(
            flops=LONG,
            bytes_accessed=2 * (groups * row_count + fine_count) * feat_dim,
            transcendentals=0,
        ),
    )(share, all_rows, old_fine, fine_norms)


def place_kernel(at_ref, *refs):
    *pieces, out_ref = refs
    for i, piece in enumerate(pieces):
        row = pl.multiple_of(at_ref[i], piece.shape[0])
        out_ref[pl.ds(row, piece.shape[0]), :] = piece[...]


def all_blocks(block, total):
    places = lax.axis_size("grp")
    cores = places // SIDE
    onward = ring(places, cores, 1)
    backward = ring(places, cores, SIDE - 1)
    across = [(i, i ^ 1) for i in range(places)]
    rows = block.shape[0]
    half = rows // 2
    before = lax.ppermute(block, "grp", onward)
    after = lax.ppermute(block, "grp", backward)
    far_first = lax.ppermute(before[:half], "grp", onward)
    far_last = lax.ppermute(after[half:], "grp", backward)
    pieces = [block, before, after, far_first, far_last]
    pieces += [lax.ppermute(piece, "grp", across) for piece in pieces]
    me = lax.axis_index("grp")
    chip = me // cores
    starts = []
    for core in (me % cores, 1 - me % cores):
        for turn, shift in ((0, 0), (SIDE - 1, 0), (1, 0), (2, 0), (2, half)):
            starts.append(((chip + turn) % SIDE * cores + core) * rows + shift)
    return pl.pallas_call(
        place_kernel,
        out_shape=jax.ShapeDtypeStruct((total, block.shape[1]), block.dtype),
        grid_spec=pltpu.PrefetchScalarGridSpec(
            num_scalar_prefetch=1,
            grid=(1,),
            in_specs=[pl.BlockSpec(piece.shape, lambda i, at: (0, 0)) for piece in pieces],
            out_specs=pl.BlockSpec((total, block.shape[1]), lambda i, at: (0, 0)),
        ),
        compiler_params=pltpu.CompilerParams(vmem_limit_bytes=32 * 1024 * 1024),
        cost_estimate=pl.CostEstimate(flops=0, bytes_accessed=4 * 1024 * 1024, transcendentals=0),
    )(jnp.stack(starts).astype(jnp.int32), *pieces)


def per_device(
    points, point_cluster, candidates, old_fine, fine_parent, old_middle, middle_parent, old_top
):
    devices = lax.axis_size(BOTH)
    group_width = lax.axis_size("sub")
    share = lax.axis_index("sub")
    device = lax.axis_index(BOTH)
    row_count, feat_dim = points.shape
    fine_count = old_fine.shape[0]
    middle_count = old_middle.shape[0]
    top_count = old_top.shape[0]
    share_rows = middle_count // group_width
    top_rows = top_count // devices
    which = jnp.stack([share, jnp.int32(group_width), jnp.int32(top_rows.bit_length() - 1)])

    slot_count = CAP + 1
    send_rows, wide_rows, middle_members = outgoing(
        which,
        point_cluster,
        points,
        middle_parent,
        fine_parent,
        candidates,
        devices,
        fine_count,
    )
    got = swap(send_rows.reshape(devices, slot_count, feat_dim), BOTH)
    side = got[:, CAP, :LANES].astype(jnp.float32)
    got_high = side[:, :CAP].astype(jnp.int32)
    got_low = side[:, LOW_LANE : LOW_LANE + CAP].astype(jnp.int32)
    got_ids = jnp.where(got_high > 0, (got_high - 1) * (1 << ID_BITS) + got_low, -1)
    got_ids = jnp.pad(got_ids, ((0, 0), (0, 1)), constant_values=-1)
    top_totals = jnp.sum(side[:, COUNT_LANE : COUNT_LANE + top_rows], axis=0)

    all_rows = lax.all_gather(wide_rows, "sub", axis=0, tiled=True)
    for apart in (1, SIDE):
        around = [middle_members]
        for turn in range(1, SIDE):
            around.append(lax.ppermute(middle_members, "sub", ring(group_width, apart, turn)))
        middle_members = sum(around)

    middle_local = fine_parent - lax.axis_index("grp") * middle_count
    got = got.reshape(devices * slot_count, feat_dim)
    got_ids = got_ids.reshape(1, devices * slot_count)
    got_ids, middle_members = lax.optimization_barrier((got_ids, middle_members))
    parents = middle_local[None, :]
    half_fine, left = left_levels(got, got_ids, old_fine, parents, middle_count)
    new_fine, right, top_part = right_levels(
        which,
        got,
        got_ids,
        old_fine,
        parents,
        middle_members,
        old_middle,
        middle_parent[None, :],
        left,
        half_fine,
        top_count,
    )

    left = swap(left.reshape(group_width, share_rows, -1), "sub")
    right, left = lax.optimization_barrier((right, left))
    right = swap(right.reshape(group_width, share_rows, -1), "sub")
    wide_fine = old_fine.astype(jnp.float32)
    fine_norms = jnp.sum(wide_fine * wide_fine, axis=1)[None, :]
    found = candidate_parts(which, all_rows, old_fine, fine_norms, group_width)
    right, found = lax.optimization_barrier((right, found))
    share_totals = lax.dynamic_slice_in_dim(middle_members, share, 1).reshape(share_rows)
    old_share = lax.dynamic_slice_in_dim(old_middle, share * share_rows, share_rows)
    left_share, right_share = [
        level_update(jnp.sum(parts.astype(jnp.float32), axis=0), share_totals, olds)
        for parts, olds in zip((left, right), jnp.split(old_share, [feat_dim // 8 * LEFT_EIGHTHS], axis=1))
    ]
    new_share = jnp.concatenate([left_share, right_share], axis=1)
    new_middle = copied(lax.all_gather(new_share, "sub", axis=0, tiled=True))

    top_block = lax.psum_scatter(top_part, "grp", scatter_dimension=0, tiled=True)
    top_pieces = top_block.reshape(group_width, top_rows, feat_dim)
    returned = swap(jnp.concatenate([top_pieces, found], axis=2), "sub")
    top_sums = jnp.sum(returned[:, :, :feat_dim], axis=0)
    packed = returned[:, :, feat_dim:].reshape(group_width, SUBLANES, -1, group_width)
    packed = packed[..., : row_count // SUBLANES]
    candidate_sq_distance = packed.transpose(3, 1, 2, 0).reshape(row_count, -1)
    old_rows = lax.dynamic_slice_in_dim(old_top, device * top_rows, top_rows)
    new_rows = level_update(top_sums, top_totals, old_rows)
    new_block = spread(new_rows, "sub").reshape(group_width * top_rows, feat_dim)
    new_top = all_blocks(new_block, top_count)
    return (new_fine, new_middle, new_top, candidate_sq_distance)


def solution(mesh):
    placed = (
        P(BOTH, None),
        P(BOTH),
        P(BOTH, None),
        P(BOTH, None),
        P(BOTH),
        P("grp", None),
        P("grp"),
        P(),
    )
    return jax.shard_map(
        per_device,
        mesh=mesh,
        in_specs=placed,
        out_specs=(P(BOTH, None), P("grp", None), P(), P(BOTH, None)),
        check_vma=False,
    )
```
